32 devices in a mesh: replica: 8 (over y, x, core), fsdp: 4 (over z).
Axes of the slice: x: 2, y: 2, z: 4, core: 2. Of those that a mesh axis runs over, the one named last changes fastest.
Arguments:
- weights: bfloat16 [8, 4096, 512], P('replica', 'fsdp'), may hold values from -6 to 6
- pseudo_grad: bfloat16 [8, 4096, 512], P('replica', 'fsdp'), may hold values from -6 to 6
- momentum: bfloat16 [8, 4096, 512], P('replica', 'fsdp'), may hold values from -6 to 6
- partner: int32 [8], replicated, may hold values from 0 to 7, as said below
- activations: bfloat16 [8192, 4096], P('replica', 'fsdp'), may hold values from -6 to 6
- key_cotangent: bfloat16 [8192, 512], P(('replica', 'fsdp')), may hold values from -0.1875 to 0.1875
Outputs:
- new_weights: bfloat16 [8, 4096, 512], P('replica', 'fsdp')
- new_momentum: bfloat16 [8, 4096, 512], P('replica', 'fsdp')
- weight_grad: bfloat16 [8, 4096, 512], P('replica', 'fsdp')
The draws below stay inside these ranges and needn't reach their ends.
Inputs may be any that keep to these rules, and one draw needn't show every extreme that they name: partner is a matching: partner[partner[r]] = r and partner[r] != r for every replica r.
All inputs are finite; a program needn't handle non-finite values.
Results may differ from the reference program's by a relative error of at most 0.001.
Values may be sent and summed in bfloat16 or wider, within the bound.
A program may use at most 64 MiB of HBM per device.

```python
import jax
import jax.numpy as jnp
from jax import lax

D = 4096
KW = 512
TOK_REP = 1024
TOKENS = 8192
N_REPLICA = 8


def draw_partner(key, part):
    key = jax.random.fold_in(key, 11)
    order = jax.random.permutation(key, N_REPLICA).astype(jnp.int32)
    first_half = order[0::2]
    second_half = order[1::2]
    matched = jnp.zeros((N_REPLICA,), jnp.int32)
    matched = matched.at[first_half].set(second_half)
    matched = matched.at[second_half].set(first_half)
    return matched


def levels(own_key, dims, pieces, least, top_value):
    factor_of, own = 1.0, jax.random.fold_in(own_key, 6)
    for axis_at, blocks in pieces:
        heights = jnp.exp(jax.random.uniform(jax.random.fold_in(own, axis_at), (blocks,), jnp.float32, least / len(pieces), top_value / len(pieces)))
        factor_of = factor_of * jnp.repeat(heights, dims[axis_at] // blocks).reshape([-1 if axis == axis_at else 1 for axis in range(len(dims))])
    return factor_of


def normal_values(key, extent, width, limit, shards=(), dtype=jnp.bfloat16):
    values = width * jax.random.normal(key, extent, jnp.float32)
    if shards:
        values = values * levels(key, extent, shards, -0.22, 0.18)
    return jnp.clip(values, -limit, limit).astype(dtype)


def setup_inputs(seed: int = 0) -> dict:
    keys = jax.random.split(jax.random.key(seed), 7)
    return {
        "weights": normal_values(keys[0], (N_REPLICA, D, KW), 1.0, 6.0, ((0, 8), (1, 4))),
        "pseudo_grad": normal_values(keys[1], (N_REPLICA, D, KW), 1.0, 6.0, ((0, 8), (1, 4))),
        "momentum": normal_values(keys[2], (N_REPLICA, D, KW), 1.0, 6.0, ((0, 8), (1, 4))),
        "partner": draw_partner(jax.random.fold_in(keys[6], 71), 0),
        "activations": normal_values(keys[4], (TOKENS, D), 1.0, 6.0, ((0, 8), (1, 4))),
        "key_cotangent": normal_values(keys[5], (TOKENS, KW), (TOK_REP ** -0.5), 0.1875, ((0, 32),)),
    }


decay_old = 0.5
grad_rate = 0.7
pull_rate = 0.9

def replica_grad(operands):
    inputs_rep, cotan_rep = operands
    return lax.dot_general(inputs_rep, cotan_rep, (((0,), (0,)), ((), ())), preferred_element_type=jnp.float32).astype(jnp.bfloat16)

def reference(weights, pseudo_grad, momentum, partner, activations, key_cotangent):
    partner_weights = jnp.take(weights, partner, axis=0)
    partner_grad = jnp.take(pseudo_grad, partner, axis=0)
    weights_f32 = weights.astype(jnp.float32)
    mean_weights = (weights_f32 + partner_weights.astype(jnp.float32)) * 0.5
    mean_grad = (pseudo_grad.astype(jnp.float32) + partner_grad.astype(jnp.float32)) * 0.5
    momentum_f = decay_old * momentum.astype(jnp.float32) - grad_rate * mean_grad - pull_rate * (weights_f32 - mean_weights)
    new_weights = (weights_f32 + decay_old * momentum_f - grad_rate * mean_grad).astype(jnp.bfloat16)
    new_momentum = momentum_f.astype(jnp.bfloat16)
    inputs_all = activations.reshape(N_REPLICA, TOK_REP, D)
    cotan_all = key_cotangent.reshape(N_REPLICA, TOK_REP, KW)
    weight_grad = lax.map(replica_grad, (inputs_all, cotan_all))
    return (new_weights, new_momentum, weight_grad)
```

```python
import functools

import jax
import jax.numpy as jnp
from jax import lax
from jax.experimental import pallas as pl
from jax.experimental.pallas import tpu as pltpu
from jax.sharding import PartitionSpec as P

CHUNKS = 4
ROW_TILE = 16
MIB = 1 << 20

decay_old = 0.5
grad_rate = 0.7
pull_rate = 0.9


def remote(src, dst, send_sem, recv_sem, **where):
    return pltpu.make_async_remote_copy(
        src_ref=src,
        dst_ref=dst,
        send_sem=send_sem,
        recv_sem=recv_sem,
        device_id=where,
        device_id_type=pl.DeviceIdType.MESH,
    )


def kernel(n, p, chunks, partner, weights, grad, momentum, acts, cotan,
           new_weights, new_momentum, weight_grad, *scratch):
    holds = scratch[:chunks]
    (routed, arrived, w_v, g_v, m_v, a_v, k_v, nw_v, nm_v, wg_v,
     spread_send, spread_recv, collect_send, collect_recv,
     k_send, k_recv, local_sem, self_sem, out_sem) = scratch[chunks:]
    me = lax.axis_index("replica")
    mz = lax.axis_index("fsdp")
    tok = cotan.shape[0]
    pieces = (weights, grad)

    barrier = pltpu.get_barrier_semaphore()

    @pl.loop(1, n)
    def _(d):
        pl.semaphore_signal(barrier, inc=1, device_id={"replica": lax.rem(me + d, n)},
                            device_id_type=pl.DeviceIdType.MESH)

    @pl.loop(1, p)
    def _(d):
        pl.semaphore_signal(barrier, inc=1, device_id={"fsdp": lax.rem(mz + d, p)},
                            device_id_type=pl.DeviceIdType.MESH)

    self_copies = []
    for c in range(chunks):
        for i in range(2):
            cp = pltpu.make_async_copy(pieces[i].at[me, c], holds[c].at[i, me], self_sem.at[c, i])
            cp.start()
            self_copies.append(cp)
    k_rows = pl.ds(pl.multiple_of(mz * tok, tok), tok)
    local_copies = [
        pltpu.make_async_copy(cotan, k_v.at[k_rows], local_sem.at[0]),
        pltpu.make_async_copy(weights, w_v, local_sem.at[1]),
        pltpu.make_async_copy(grad, g_v, local_sem.at[2]),
        pltpu.make_async_copy(momentum, m_v, local_sem.at[3]),
        pltpu.make_async_copy(acts, a_v, local_sem.at[4]),
    ]
    for cp in local_copies:
        cp.start()

    pl.semaphore_wait(barrier, n - 1 + p - 1)

    def spread(c, i, to):
        return remote(pieces[i].at[to, c], holds[c].at[i, me],
                      spread_send.at[c, i, to], spread_recv.at[c, i, me], replica=to)

    def spread_in(c, i, frm):
        return remote(pieces[i].at[frm, c], holds[c].at[i, frm],
                      spread_send.at[c, i, frm], spread_recv.at[c, i, frm], replica=frm)

    def collect(c, to):
        return remote(routed.at[c, to], arrived.at[c, me],
                      collect_send.at[c, to], collect_recv.at[c, me], replica=to)

    def collect_in(c, frm):
        return remote(routed.at[c, frm], arrived.at[c, frm],
                      collect_send.at[c, frm], collect_recv.at[c, frm], replica=frm)

    def share(to):
        return remote(cotan, k_v.at[k_rows], k_send.at[to], k_recv.at[mz], fsdp=to)

    def share_in(frm):
        rows = pl.ds(pl.multiple_of(frm * tok, tok), tok)
        return remote(cotan, k_v.at[rows], k_send.at[frm], k_recv.at[frm], fsdp=frm)

    for c in range(chunks):
        @pl.loop(1, n)
        def _(d, c=c):
            to = lax.rem(me + d, n)
            spread(c, 0, to).start()
            spread(c, 1, to).start()

        if c == 0:
            @pl.loop(1, p)
            def _(d):
                share(lax.rem(mz + d, p)).start()

    for c in range(chunks):
        self_copies[2 * c].wait()
        self_copies[2 * c + 1].wait()

        @pl.loop(1, n)
        def _(d, c=c):
            frm = lax.rem(me + n - d, n)
            spread_in(c, 0, frm).wait_recv()
            spread_in(c, 1, frm).wait_recv()

        @pl.loop(1, n)
        def _(d, c=c):
            to = lax.rem(me + d, n)
            source = partner[to]
            routed[c, to, 0] = holds[c][0, source]
            routed[c, to, 1] = holds[c][1, source]
            collect(c, to).start()

        source = partner[me]
        arrived[c, me, 0] = holds[c][0, source]
        arrived[c, me, 1] = holds[c][1, source]

    for cp in local_copies:
        cp.wait()

    @pl.loop(1, p)
    def _(d):
        share_in(lax.rem(mz + p - d, p)).wait_recv()

    feats = a_v.shape[1]
    step = 256 if feats % 256 == 0 else feats

    @pl.loop(0, feats // step)
    def _(t):
        cols = pl.ds(pl.multiple_of(t * step, step), step)
        wg_v[cols, :] = lax.dot_general(
            a_v[:, cols], k_v[...], (((0,), (0,)), ((), ())),
            preferred_element_type=jnp.float32).astype(wg_v.dtype)

    wg_out = pltpu.make_async_copy(wg_v, weight_grad, out_sem.at[2, 0])
    wg_out.start()

    out_copies = [wg_out]
    for c in range(chunks):
        @pl.loop(0, n)
        def _(d, c=c):
            frm = lax.rem(me + n - d, n)

            @pl.when(d > 0)
            def _():
                collect_in(c, frm).wait_recv()

            w = w_v[frm, c].astype(jnp.float32)
            g = g_v[frm, c].astype(jnp.float32)
            mean_w = (w + arrived[c, frm, 0].astype(jnp.float32)) * 0.5
            mean_g = (g + arrived[c, frm, 1].astype(jnp.float32)) * 0.5
            mom = (decay_old * m_v[frm, c].astype(jnp.float32)
                   - grad_rate * mean_g - pull_rate * (w - mean_w))
            nw_v[frm, c] = (w + decay_old * mom - grad_rate * mean_g).astype(nw_v.dtype)
            nm_v[frm, c] = mom.astype(nm_v.dtype)

        for i, (src, dst) in enumerate(((nw_v, new_weights), (nm_v, new_momentum))):
            cp = pltpu.make_async_copy(src.at[:, c], dst.at[:, c], out_sem.at[i, c])
            cp.start()
            out_copies.append(cp)

    for c in range(chunks):
        @pl.loop(1, n)
        def _(d, c=c):
            to = lax.rem(me + d, n)
            spread(c, 0, to).wait_send()
            spread(c, 1, to).wait_send()
            collect(c, to).wait_send()

    @pl.loop(1, p)
    def _(d):
        share(lax.rem(mz + d, p)).wait_send()

    for cp in out_copies:
        cp.wait()


def on_device(weights, pseudo_grad, momentum, partner, activations, key_cotangent):
    n, p = lax.axis_size("replica"), lax.axis_size("fsdp")
    rows, cols = weights.shape[1:]
    chunks = CHUNKS if rows >= n * CHUNKS * ROW_TILE else 1
    piece = -(-rows // (n * chunks * ROW_TILE)) * ROW_TILE
    padded = n * chunks * piece
    view = (n, chunks, piece, cols)

    def cut(x):
        x = x[0]
        if padded != rows:
            x = jnp.pad(x, ((0, padded - rows), (0, 0)))
        return x.reshape(view)

    def join(x):
        return x.reshape(padded, cols)[:rows][None]

    bf16 = jnp.bfloat16
    tokens, feats = activations.shape
    out_view = jax.ShapeDtypeStruct(view, bf16)
    any_space = pl.BlockSpec(memory_space=pl.ANY)
    dma = pltpu.SemaphoreType.DMA
    new_weights, new_momentum, weight_grad = pl.pallas_call(
        functools.partial(kernel, n, p, chunks),
        out_shape=(out_view, out_view, jax.ShapeDtypeStruct((feats, cols), bf16)),
        in_specs=[pl.BlockSpec(memory_space=pltpu.SMEM)] + [any_space] * 5,
        out_specs=(any_space,) * 3,
        scratch_shapes=[pltpu.VMEM((2, n, piece, cols), bf16) for _ in range(chunks)] + [
            pltpu.VMEM((chunks, n, 2, piece, cols), bf16),
            pltpu.VMEM((chunks, n, 2, piece, cols), bf16),
            pltpu.VMEM(view, bf16),
            pltpu.VMEM(view, bf16),
            pltpu.VMEM(view, bf16),
            pltpu.VMEM((tokens, feats), bf16),
            pltpu.VMEM((tokens, cols), bf16),
            pltpu.VMEM(view, bf16),
            pltpu.VMEM(view, bf16),
            pltpu.VMEM((feats, cols), bf16),
            dma((chunks, 2, n)),
            dma((chunks, 2, n)),
            dma((chunks, n)),
            dma((chunks, n)),
            dma((p,)),
            dma((p,)),
            dma((5,)),
            dma((chunks, 2)),
            dma((3, chunks)),
        ],
        compiler_params=pltpu.CompilerParams(
            collective_id=0, has_side_effects=True, vmem_limit_bytes=48 * MIB),
        cost_estimate=pl.CostEstimate(
            flops=2 * tokens * feats * cols, bytes_accessed=20 * rows * cols, transcendentals=0),
    )(partner, cut(weights), cut(pseudo_grad), cut(momentum), activations, key_cotangent)
    return join(new_weights), join(new_momentum), weight_grad[None]


def solution(mesh):
    return jax.shard_map(
        on_device,
        mesh=mesh,
        in_specs=(
            P("replica", "fsdp", None),
            P("replica", "fsdp", None),
            P("replica", "fsdp", None),
            P(),
            P("replica", "fsdp"),
            P(("replica", "fsdp"), None),
        ),
        out_specs=(
            P("replica", "fsdp", None),
            P("replica", "fsdp", None),
            P("replica", "fsdp", None),
        ),
        check_vma=False,
    )
```

```python
import functools

import jax
import jax.numpy as jnp
from jax import lax
from jax.experimental import pallas as pl
from jax.experimental.pallas import tpu as pltpu
from jax.sharding import PartitionSpec as P

CHUNKS = 4
ROW_TILE = 16
MIB = 1 << 20

decay_old = 0.5
grad_rate = 0.7
pull_rate = 0.9


def remote(src, dst, send_sem, recv_sem, **where):
    return pltpu.make_async_remote_copy(
        src_ref=src,
        dst_ref=dst,
        send_sem=send_sem,
        recv_sem=recv_sem,
        device_id=where,
        device_id_type=pl.DeviceIdType.MESH,
    )


def kernel(n, p, chunks, partner, weights, grad, momentum, acts, cotan,
           new_weights, new_momentum, weight_grad, *scratch):
    holds = scratch[:chunks]
    (routed, arrived, w_v, g_v, m_v, a_v, k_v, nw_v, nm_v, wg_v,
     spread_send, spread_recv, collect_send, collect_recv,
     k_send, k_recv, local_sem, self_sem, out_sem) = scratch[chunks:]
    me = lax.axis_index("replica")
    mz = lax.axis_index("fsdp")
    tok = cotan.shape[0]
    pieces = (weights, grad)

    barrier = pltpu.get_barrier_semaphore()

    @pl.loop(1, n)
    def _(d):
        pl.semaphore_signal(barrier, inc=1, device_id={"replica": lax.rem(me + d, n)},
                            device_id_type=pl.DeviceIdType.MESH)

    @pl.loop(1, p)
    def _(d):
        pl.semaphore_signal(barrier, inc=1, device_id={"fsdp": lax.rem(mz + d, p)},
                            device_id_type=pl.DeviceIdType.MESH)

    self_copies = []
    for c in range(chunks):
        for i in range(2):
            cp = pltpu.make_async_copy(pieces[i].at[me, c], holds[c].at[i, me], self_sem.at[c, i])
            cp.start()
            self_copies.append(cp)
    k_rows = pl.ds(pl.multiple_of(mz * tok, tok), tok)
    local_copies = [
        pltpu.make_async_copy(cotan, k_v.at[k_rows], local_sem.at[0]),
        pltpu.make_async_copy(weights, w_v, local_sem.at[1]),
        pltpu.make_async_copy(grad, g_v, local_sem.at[2]),
        pltpu.make_async_copy(momentum, m_v, local_sem.at[3]),
        pltpu.make_async_copy(acts, a_v, local_sem.at[4]),
    ]
    for cp in local_copies:
        cp.start()

    pl.semaphore_wait(barrier, n - 1 + p - 1)

    def spread(c, i, to):
        return remote(pieces[i].at[to, c], holds[c].at[i, me],
                      spread_send.at[c, i, to], spread_recv.at[c, i, me], replica=to)

    def spread_in(c, i, frm):
        return remote(pieces[i].at[frm, c], holds[c].at[i, frm],
                      spread_send.at[c, i, frm], spread_recv.at[c, i, frm], replica=frm)

    def collect(c, to):
        return remote(routed.at[c, to], arrived.at[c, me],
                      collect_send.at[c, to], collect_recv.at[c, me], replica=to)

    def collect_in(c, frm):
        return remote(routed.at[c, frm], arrived.at[c, frm],
                      collect_send.at[c, frm], collect_recv.at[c, frm], replica=frm)

    def share(to):
        return remote(cotan, k_v.at[k_rows], k_send.at[to], k_recv.at[mz], fsdp=to)

    def share_in(frm):
        rows = pl.ds(pl.multiple_of(frm * tok, tok), tok)
        return remote(cotan, k_v.at[rows], k_send.at[frm], k_recv.at[frm], fsdp=frm)

    for c in range(chunks):
        @pl.loop(1, n)
        def _(d, c=c):
            to = lax.rem(me + d, n)
            spread(c, 0, to).start()
            spread(c, 1, to).start()

        if c == 0:
            @pl.loop(1, p)
            def _(d):
                share(lax.rem(mz + d, p)).start()

    for c in range(chunks):
        self_copies[2 * c].wait()
        self_copies[2 * c + 1].wait()

        @pl.loop(1, n)
        def _(d, c=c):
            frm = lax.rem(me + n - d, n)
            spread_in(c, 0, frm).wait_recv()
            spread_in(c, 1, frm).wait_recv()

        @pl.loop(1, n)
        def _(d, c=c):
            to = lax.rem(me + d, n)
            source = partner[to]
            routed[c, to, 0] = holds[c][0, source]
            routed[c, to, 1] = holds[c][1, source]
            collect(c, to).start()

        source = partner[me]
        arrived[c, me, 0] = holds[c][0, source]
        arrived[c, me, 1] = holds[c][1, source]

    for cp in local_copies:
        cp.wait()

    @pl.loop(1, p)
    def _(d):
        share_in(lax.rem(mz + p - d, p)).wait_recv()

    feats = a_v.shape[1]
    step = 256 if feats % 256 == 0 else feats

    @pl.loop(0, feats // step)
    def _(t):
        cols = pl.ds(pl.multiple_of(t * step, step), step)
        wg_v[cols, :] = lax.dot_general(
            a_v[:, cols], k_v[...], (((0,), (0,)), ((), ())),
            preferred_element_type=jnp.float32).astype(wg_v.dtype)

    wg_out = pltpu.make_async_copy(wg_v, weight_grad, out_sem.at[2, 0])
    wg_out.start()

    out_copies = [wg_out]
    for c in range(chunks):
        @pl.loop(0, n)
        def _(d, c=c):
            frm = lax.rem(me + n - d, n)

            @pl.when(d > 0)
            def _():
                collect_in(c, frm).wait_recv()

            w = w_v[frm, c].astype(jnp.float32)
            g = g_v[frm, c].astype(jnp.float32)
            mean_w = (w + arrived[c, frm, 0].astype(jnp.float32)) * 0.5
            mean_g = (g + arrived[c, frm, 1].astype(jnp.float32)) * 0.5
            mom = (decay_old * m_v[frm, c].astype(jnp.float32)
                   - grad_rate * mean_g - pull_rate * (w - mean_w))
            nw_v[frm, c] = (w + decay_old * mom - grad_rate * mean_g).astype(nw_v.dtype)
            nm_v[frm, c] = mom.astype(nm_v.dtype)

        for i, (src, dst) in enumerate(((nw_v, new_weights), (nm_v, new_momentum))):
            cp = pltpu.make_async_copy(src.at[:, c], dst.at[:, c], out_sem.at[i, c])
            cp.start()
            out_copies.append(cp)

    for c in range(chunks):
        @pl.loop(1, n)
        def _(d, c=c):
            to = lax.rem(me + d, n)
            spread(c, 0, to).wait_send()
            spread(c, 1, to).wait_send()
            collect(c, to).wait_send()

    @pl.loop(1, p)
    def _(d):
        share(lax.rem(mz + d, p)).wait_send()

    for cp in out_copies:
        cp.wait()


def on_device(weights, pseudo_grad, momentum, partner, activations, key_cotangent):
    n, p = lax.axis_size("replica"), lax.axis_size("fsdp")
    rows, cols = weights.shape[1:]
    chunks = CHUNKS if rows >= n * CHUNKS * ROW_TILE else 1
    piece = -(-rows // (n * chunks * ROW_TILE)) * ROW_TILE
    padded = n * chunks * piece
    view = (n, chunks, piece, cols)

    def cut(x):
        x = x[0]
        if padded != rows:
            x = jnp.pad(x, ((0, padded - rows), (0, 0)))
        return x.reshape(view)

    def join(x):
        return x.reshape(padded, cols)[:rows][None]

    bf16 = jnp.bfloat16
    tokens, feats = activations.shape
    out_view = jax.ShapeDtypeStruct(view, bf16)
    any_space = pl.BlockSpec(memory_space=pl.ANY)
    dma = pltpu.SemaphoreType.DMA
    new_weights, new_momentum, weight_grad = pl.pallas_call(
        functools.partial(kernel, n, p, chunks),
        out_shape=(out_view, out_view, jax.ShapeDtypeStruct((feats, cols), bf16)),
        in_specs=[pl.BlockSpec(memory_space=pltpu.SMEM)] + [any_space] * 5,
        out_specs=(any_space,) * 3,
        scratch_shapes=[pltpu.VMEM((2, n, piece, cols), bf16) for _ in range(chunks)] + [
            pltpu.VMEM((chunks, n, 2, piece, cols), bf16),
            pltpu.VMEM((chunks, n, 2, piece, cols), bf16),
            pltpu.VMEM(view, bf16),
            pltpu.VMEM(view, bf16),
            pltpu.VMEM(view, bf16),
            pltpu.VMEM((tokens, feats), bf16),
            pltpu.VMEM((tokens, cols), bf16),
            pltpu.VMEM(view, bf16),
            pltpu.VMEM(view, bf16),
            pltpu.VMEM((feats, cols), bf16),
            dma((chunks, 2, n)),
            dma((chunks, 2, n)),
            dma((chunks, n)),
            dma((chunks, n)),
            dma((p,)),
            dma((p,)),
            dma((5,)),
            dma((chunks, 2)),
            dma((3, chunks)),
        ],
        compiler_params=pltpu.CompilerParams(
            collective_id=0, has_side_effects=True, vmem_limit_bytes=62 * MIB),
        cost_estimate=pl.CostEstimate(
            flops=2 * tokens * feats * cols, bytes_accessed=20 * rows * cols, transcendentals=0),
    )(partner, cut(weights), cut(pseudo_grad), cut(momentum), activations, key_cotangent)
    return join(new_weights), join(new_momentum), weight_grad[None]


def solution(mesh):
    return jax.shard_map(
        on_device,
        mesh=mesh,
        in_specs=(
            P("replica", "fsdp", None),
            P("replica", "fsdp", None),
            P("replica", "fsdp", None),
            P(),
            P("replica", "fsdp"),
            P(("replica", "fsdp"), None),
        ),
        out_specs=(
            P("replica", "fsdp", None),
            P("replica", "fsdp", None),
            P("replica", "fsdp", None),
        ),
        check_vma=False,
    )
```

```python
import functools

import jax
import jax.numpy as jnp
from jax import lax
from jax.experimental import pallas as pl
from jax.experimental.pallas import tpu as pltpu
from jax.sharding import PartitionSpec as P

CHUNKS = 4
LANE_CHUNKS = 16
ROW_TILE = 16
MIB = 1 << 20

decay_old = 0.5
grad_rate = 0.7
pull_rate = 0.9


def remote(src, dst, send_sem, recv_sem, **where):
    return pltpu.make_async_remote_copy(
        src_ref=src,
        dst_ref=dst,
        send_sem=send_sem,
        recv_sem=recv_sem,
        device_id=where,
        device_id_type=pl.DeviceIdType.MESH,
    )


def update(w, g, m, partner_w, partner_g):
    f32 = jnp.float32
    w, g = w.astype(f32), g.astype(f32)
    mean_w = (w + partner_w.astype(f32)) * 0.5
    mean_g = (g + partner_g.astype(f32)) * 0.5
    mom = decay_old * m.astype(f32) - grad_rate * mean_g - pull_rate * (w - mean_w)
    new_w = w + decay_old * mom - grad_rate * mean_g
    return new_w.astype(jnp.bfloat16), mom.astype(jnp.bfloat16)


def multiply(a_v, k_v, wg_v):
    feats = a_v.shape[1]
    step = 256 if feats % 256 == 0 else feats

    @pl.loop(0, feats // step)
    def _(t):
        cols = pl.ds(pl.multiple_of(t * step, step), step)
        wg_v[cols, :] = lax.dot_general(
            a_v[:, cols], k_v[...], (((0,), (0,)), ((), ())),
            preferred_element_type=jnp.float32).astype(wg_v.dtype)


def kernel(n, p, chunks, partner, weights, grad, momentum, acts, cotan,
           new_weights, new_momentum, weight_grad, *scratch):
    holds = scratch[:chunks]
    (routed, arrived, w_v, g_v, m_v, a_v, k_v, nw_v, nm_v, wg_v,
     spread_send, spread_recv, collect_send, collect_recv,
     k_send, k_recv, local_sem, self_sem, out_sem) = scratch[chunks:]
    me = lax.axis_index("replica")
    mz = lax.axis_index("fsdp")
    tok = cotan.shape[0]
    pieces = (weights, grad)

    barrier = pltpu.get_barrier_semaphore()

    @pl.loop(1, n)
    def _(d):
        pl.semaphore_signal(barrier, inc=1, device_id={"replica": lax.rem(me + d, n)},
                            device_id_type=pl.DeviceIdType.MESH)

    @pl.loop(1, p)
    def _(d):
        pl.semaphore_signal(barrier, inc=1, device_id={"fsdp": lax.rem(mz + d, p)},
                            device_id_type=pl.DeviceIdType.MESH)

    self_copies = []
    for c in range(chunks):
        for i in range(2):
            cp = pltpu.make_async_copy(pieces[i].at[me, c], holds[c].at[i, me], self_sem.at[c, i])
            cp.start()
            self_copies.append(cp)
    k_rows = pl.ds(pl.multiple_of(mz * tok, tok), tok)
    local_copies = [
        pltpu.make_async_copy(cotan, k_v.at[k_rows], local_sem.at[0]),
        pltpu.make_async_copy(weights, w_v, local_sem.at[1]),
        pltpu.make_async_copy(grad, g_v, local_sem.at[2]),
        pltpu.make_async_copy(momentum, m_v, local_sem.at[3]),
        pltpu.make_async_copy(acts, a_v, local_sem.at[4]),
    ]
    for cp in local_copies:
        cp.start()

    pl.semaphore_wait(barrier, n - 1 + p - 1)

    def spread(c, i, to):
        return remote(pieces[i].at[to, c], holds[c].at[i, me],
                      spread_send.at[c, i, to], spread_recv.at[c, i, me], replica=to)

    def spread_in(c, i, frm):
        return remote(pieces[i].at[frm, c], holds[c].at[i, frm],
                      spread_send.at[c, i, frm], spread_recv.at[c, i, frm], replica=frm)

    def collect(c, to):
        return remote(routed.at[c, to], arrived.at[c, me],
                      collect_send.at[c, to], collect_recv.at[c, me], replica=to)

    def collect_in(c, frm):
        return remote(routed.at[c, frm], arrived.at[c, frm],
                      collect_send.at[c, frm], collect_recv.at[c, frm], replica=frm)

    def share(to):
        return remote(cotan, k_v.at[k_rows], k_send.at[to], k_recv.at[mz], fsdp=to)

    def share_in(frm):
        rows = pl.ds(pl.multiple_of(frm * tok, tok), tok)
        return remote(cotan, k_v.at[rows], k_send.at[frm], k_recv.at[frm], fsdp=frm)

    for c in range(chunks):
        @pl.loop(1, n)
        def _(d, c=c):
            to = lax.rem(me + d, n)
            spread(c, 0, to).start()
            spread(c, 1, to).start()

        if c == 0:
            @pl.loop(1, p)
            def _(d):
                share(lax.rem(mz + d, p)).start()

    for c in range(chunks):
        self_copies[2 * c].wait()
        self_copies[2 * c + 1].wait()

        @pl.loop(1, n)
        def _(d, c=c):
            frm = lax.rem(me + n - d, n)
            spread_in(c, 0, frm).wait_recv()
            spread_in(c, 1, frm).wait_recv()

        @pl.loop(1, n)
        def _(d, c=c):
            to = lax.rem(me + d, n)
            source = partner[to]
            routed[c, to, 0] = holds[c][0, source]
            routed[c, to, 1] = holds[c][1, source]
            collect(c, to).start()

        source = partner[me]
        arrived[c, me, 0] = holds[c][0, source]
        arrived[c, me, 1] = holds[c][1, source]

    for cp in local_copies:
        cp.wait()

    @pl.loop(1, p)
    def _(d):
        share_in(lax.rem(mz + p - d, p)).wait_recv()

    multiply(a_v, k_v, wg_v)
    wg_out = pltpu.make_async_copy(wg_v, weight_grad, out_sem.at[2, 0])
    wg_out.start()

    out_copies = [wg_out]
    for c in range(chunks):
        @pl.loop(0, n)
        def _(d, c=c):
            frm = lax.rem(me + n - d, n)

            @pl.when(d > 0)
            def _():
                collect_in(c, frm).wait_recv()

            nw_v[frm, c], nm_v[frm, c] = update(
                w_v[frm, c], g_v[frm, c], m_v[frm, c], arrived[c, frm, 0], arrived[c, frm, 1])

        for i, (src, dst) in enumerate(((nw_v, new_weights), (nm_v, new_momentum))):
            cp = pltpu.make_async_copy(src.at[:, c], dst.at[:, c], out_sem.at[i, c])
            cp.start()
            out_copies.append(cp)

    for c in range(chunks):
        @pl.loop(1, n)
        def _(d, c=c):
            to = lax.rem(me + d, n)
            spread(c, 0, to).wait_send()
            spread(c, 1, to).wait_send()
            collect(c, to).wait_send()

    @pl.loop(1, p)
    def _(d):
        share(lax.rem(mz + d, p)).wait_send()

    for cp in out_copies:
        cp.wait()


def lane_kernel(p, chunks, groups, partner, weights, grad, momentum, acts, cotan,
                new_weights, new_momentum, weight_grad,
                own, rx, ry, tx, ty, handed, taken, w_v, g_v, m_v, a_v, k_v, nw_v, nm_v, wg_v,
                x_send, x_recv, y_send, y_recv, pair_send, pair_recv, hand_send, hand_recv,
                k_send, k_recv, local_sem, own_sem, out_sem):
    me = lax.axis_index("replica")
    mz = lax.axis_index("fsdp")
    core, chip = lax.rem(me, 2), lax.div(me, 2)
    x_chip = chip + 1 - 2 * lax.rem(chip, 2)
    y_chip = chip + 2 - 4 * lax.div(chip, 2)
    x_dev, y_dev, twin = 2 * x_chip + core, 2 * y_chip + core, 2 * chip + 1 - core
    tok = cotan.shape[0]
    pieces = (weights, grad)

    barrier = pltpu.get_barrier_semaphore()
    for peer in (x_dev, y_dev, twin):
        pl.semaphore_signal(barrier, inc=1, device_id={"replica": peer},
                            device_id_type=pl.DeviceIdType.MESH)

    @pl.loop(1, p)
    def _(d):
        pl.semaphore_signal(barrier, inc=1, device_id={"fsdp": lax.rem(mz + d, p)},
                            device_id_type=pl.DeviceIdType.MESH)

    def own_copy(j, i):
        at = pl.ds(groups[j][0], groups[j][1])
        return pltpu.make_async_copy(
            pieces[i].at[core, at], own.at[core, i, at], own_sem.at[j, i])

    for j in range(len(groups)):
        own_copy(j, 0).start()
        own_copy(j, 1).start()
    k_rows = pl.ds(pl.multiple_of(mz * tok, tok), tok)
    local_copies = [
        pltpu.make_async_copy(cotan, k_v.at[k_rows], local_sem.at[0]),
        pltpu.make_async_copy(weights, w_v, local_sem.at[1]),
        pltpu.make_async_copy(grad, g_v, local_sem.at[2]),
        pltpu.make_async_copy(momentum, m_v, local_sem.at[3]),
        pltpu.make_async_copy(acts, a_v, local_sem.at[4]),
    ]

    low, high = jnp.minimum(x_chip, y_chip), jnp.maximum(x_chip, y_chip)
    low_closed = partner[2 * low] == 2 * low + 1
    high_closed = partner[2 * high] == 2 * high + 1

    def route(i):
        j = partner[i]
        there = lax.div(j, 2)
        first = lax.rem(jnp.where(there < chip, j, i), 2)
        by_high = jnp.logical_and(high_closed,
                                  jnp.logical_or(jnp.logical_not(low_closed), first == 1))
        by = jnp.where(by_high, high, low)
        corner = jnp.where(by == x_chip, 3, 4)
        return jnp.where(there == chip, 0,
                         jnp.where(there == x_chip, 1, jnp.where(there == y_chip, 2, corner)))

    def starts_x(code):
        return jnp.logical_or(code == 1, code == 3)

    def starts_y(code):
        return jnp.logical_or(code == 2, code == 4)

    code0, code1 = route(2 * chip), route(2 * chip + 1)
    code_me, code_twin = route(me), route(twin)

    pl.semaphore_wait(barrier, 3 + p - 1)

    def pair(j, i):
        at = pl.ds(groups[j][0], groups[j][1])
        return remote(pieces[i].at[1 - core, at], own.at[core, i, at],
                      pair_send.at[j, i], pair_recv.at[j, i], replica=twin)

    def pair_in(j, i):
        at = pl.ds(groups[j][0], groups[j][1])
        return remote(pieces[i].at[1 - core, at], own.at[1 - core, i, at],
                      pair_send.at[j, i], pair_recv.at[j, i], replica=twin)

    def link_x(t):
        return remote(tx.at[t], rx.at[t], x_send.at[t], x_recv.at[t], replica=x_dev)

    def link_y(t):
        return remote(ty.at[t], ry.at[t], y_send.at[t], y_recv.at[t], replica=y_dev)

    def hand(c):
        return remote(handed.at[c], taken.at[c], hand_send.at[c], hand_recv.at[c], replica=twin)

    def share(to):
        return remote(cotan, k_v.at[k_rows], k_send.at[to], k_recv.at[mz], fsdp=to)

    def share_in(frm):
        rows = pl.ds(pl.multiple_of(frm * tok, tok), tok)
        return remote(cotan, k_v.at[rows], k_send.at[frm], k_recv.at[frm], fsdp=frm)

    for j in range(len(groups)):
        pair(j, 0).start()
        pair(j, 1).start()
        if j == 0:
            @pl.loop(1, p)
            def _(d):
                share(lax.rem(mz + d, p)).start()
    for cp in local_copies:
        cp.start()

    def pick(code, near, c):
        far = lax.select(code == 3, rx[c + 2], ry[c + 2])
        far = lax.select(code == 2, ry[c], far)
        far = lax.select(code == 1, rx[c], far)
        return lax.select(code == 0, near, far)

    out_copies = []

    def settle(half, c, got):
        nw_v[half, c], nm_v[half, c] = update(
            w_v[half, c], g_v[half, c], m_v[half, c], got[0], got[1])

    def finish(c):
        hand(c).wait_recv()
        settle(1 - core, c, taken[c])
        if c % 4 == 3:
            at = pl.ds(c - 3, 4)
            for i, (src, dst) in enumerate(((nw_v, new_weights), (nm_v, new_momentum))):
                cp = pltpu.make_async_copy(src.at[:, at], dst.at[:, at], out_sem.at[i, c // 4])
                cp.start()
                out_copies.append(cp)

    def deliver(c):
        handed[c] = pick(code_twin, own[core, :, c], c)
        hand(c).start()
        settle(core, c, pick(code_me, own[1 - core, :, c], c))
        if c >= 2:
            finish(c - 2)

    for t in range(chunks + 2):
        for j, (at, _) in enumerate(groups):
            if at == t:
                for i in range(2):
                    own_copy(j, i).wait()
                    pair_in(j, i).wait_recv()
        if t < chunks:
            block0, block1 = own[0, :, t], own[1, :, t]
        if t >= 2:
            link_x(t - 2).wait_recv()
            link_y(t - 2).wait_recv()
            out_x, out_y = ry[t - 2], rx[t - 2]
        else:
            out_x, out_y = block1, block1
        if t < chunks:
            out_x = lax.select(starts_x(code0), block0, lax.select(starts_x(code1), block1, out_x))
            out_y = lax.select(starts_y(code0), block0, lax.select(starts_y(code1), block1, out_y))
        tx[t] = out_x
        link_x(t).start()
        ty[t] = out_y
        link_y(t).start()
        if t == 4:
            for cp in local_copies:
                cp.wait()
        if t >= 4:
            deliver(t - 4)

    @pl.loop(1, p)
    def _(d):
        share_in(lax.rem(mz + p - d, p)).wait_recv()

    multiply(a_v, k_v, wg_v)
    wg_out = pltpu.make_async_copy(wg_v, weight_grad, out_sem.at[2, 0])
    wg_out.start()
    out_copies.append(wg_out)

    for t in (chunks, chunks + 1):
        link_x(t).wait_recv()
        link_y(t).wait_recv()
        deliver(t - 2)
    finish(chunks - 2)
    finish(chunks - 1)

    for t in range(chunks + 2):
        link_x(t).wait_send()
        link_y(t).wait_send()
    for c in range(chunks):
        hand(c).wait_send()
    for j in range(len(groups)):
        pair(j, 0).wait_send()
        pair(j, 1).wait_send()

    @pl.loop(1, p)
    def _(d):
        share(lax.rem(mz + d, p)).wait_send()

    for cp in out_copies:
        cp.wait()


def call(body, identity, view, operands, scratch):
    partner, weights, grad, momentum, acts, cotan = operands
    bf16 = jnp.bfloat16
    (tokens, feats), cols = acts.shape, cotan.shape[1]
    out_view = jax.ShapeDtypeStruct(view, bf16)
    any_space = pl.BlockSpec(memory_space=pl.ANY)
    return pl.pallas_call(
        body,
        out_shape=(out_view, out_view, jax.ShapeDtypeStruct((feats, cols), bf16)),
        in_specs=[pl.BlockSpec(memory_space=pltpu.SMEM)] + [any_space] * 5,
        out_specs=(any_space,) * 3,
        scratch_shapes=scratch,
        compiler_params=pltpu.CompilerParams(
            collective_id=identity, has_side_effects=True, vmem_limit_bytes=62 * MIB),
        cost_estimate=pl.CostEstimate(
            flops=2 * tokens * feats * cols, bytes_accessed=20 * weights.size // weights.shape[0],
            transcendentals=0),
    )(partner, weights.reshape(view), grad.reshape(view), momentum.reshape(view), acts, cotan)


def spread_form(n, p, weights, pseudo_grad, momentum, partner, activations, key_cotangent):
    rows, cols = weights.shape
    chunks = CHUNKS if rows >= n * CHUNKS * ROW_TILE else 1
    piece = -(-rows // (n * chunks * ROW_TILE)) * ROW_TILE
    padded = n * chunks * piece
    view = (n, chunks, piece, cols)

    def cut(x):
        return jnp.pad(x, ((0, padded - rows), (0, 0))) if padded != rows else x

    def join(x):
        return x.reshape(padded, cols)[:rows]

    bf16 = jnp.bfloat16
    tokens, feats = activations.shape
    dma = pltpu.SemaphoreType.DMA
    vmem = pltpu.VMEM
    scratch = [vmem((2, n, piece, cols), bf16) for _ in range(chunks)] + [
        vmem((chunks, n, 2, piece, cols), bf16), vmem((chunks, n, 2, piece, cols), bf16),
        vmem(view, bf16), vmem(view, bf16), vmem(view, bf16),
        vmem((tokens, feats), bf16), vmem((tokens, cols), bf16),
        vmem(view, bf16), vmem(view, bf16), vmem((feats, cols), bf16),
        dma((chunks, 2, n)), dma((chunks, 2, n)), dma((chunks, n)), dma((chunks, n)),
        dma((p,)), dma((p,)), dma((5,)), dma((chunks, 2)), dma((3, chunks)),
    ]
    new_weights, new_momentum, weight_grad = call(
        functools.partial(kernel, n, p, chunks), 0, view,
        (partner, cut(weights), cut(pseudo_grad), cut(momentum), activations, key_cotangent),
        scratch)
    return join(new_weights), join(new_momentum), weight_grad


def lane_form(p, weights, pseudo_grad, momentum, partner, activations, key_cotangent):
    rows, cols = weights.shape
    chunks = LANE_CHUNKS
    piece = rows // (2 * chunks)
    view = (2, chunks, piece, cols)
    groups = ((0, 1), (1, 1), (2, 2), (4, 4), (8, chunks - 8))
    bf16 = jnp.bfloat16
    tokens, feats = activations.shape
    dma = pltpu.SemaphoreType.DMA
    vmem = pltpu.VMEM
    lane = vmem((chunks + 2, 2, piece, cols), bf16)
    scratch = [
        vmem((2, 2, chunks, piece, cols), bf16), lane, lane, lane, lane,
        vmem((chunks, 2, piece, cols), bf16), vmem((chunks, 2, piece, cols), bf16),
        vmem(view, bf16), vmem(view, bf16), vmem(view, bf16),
        vmem((tokens, feats), bf16), vmem((tokens, cols), bf16),
        vmem(view, bf16), vmem(view, bf16), vmem((feats, cols), bf16),
        dma((chunks + 2,)), dma((chunks + 2,)), dma((chunks + 2,)), dma((chunks + 2,)),
        dma((len(groups), 2)), dma((len(groups), 2)), dma((chunks,)), dma((chunks,)),
        dma((p,)), dma((p,)), dma((5,)), dma((len(groups), 2)), dma((3, chunks // 4)),
    ]
    new_weights, new_momentum, weight_grad = call(
        functools.partial(lane_kernel, p, chunks, groups), 1, view,
        (partner, weights, pseudo_grad, momentum, activations, key_cotangent), scratch)
    return new_weights.reshape(rows, cols), new_momentum.reshape(rows, cols), weight_grad


def one_block_a_link(partner):
    index = lax.iota(jnp.int32, 8)
    over_x = (index // 2 + partner // 2) % 2
    over_y = (index // 4 + partner // 4) % 2
    crossings = jnp.sum(over_x + 16 * over_y)
    return (crossings == 0) | (crossings == 4 * 17)


def on_device(weights, pseudo_grad, momentum, partner, activations, key_cotangent):
    n, p = lax.axis_size("replica"), lax.axis_size("fsdp")
    operands = (weights[0], pseudo_grad[0], momentum[0], partner, activations, key_cotangent)
    spread = functools.partial(spread_form, n, p)
    if n == 8 and weights.shape[1] % (2 * LANE_CHUNKS * ROW_TILE) == 0:
        outs = lax.cond(one_block_a_link(partner), functools.partial(lane_form, p), spread,
                        *operands)
    else:
        outs = spread(*operands)
    return tuple(out[None] for out in outs)


def solution(mesh):
    return jax.shard_map(
        on_device,
        mesh=mesh,
        in_specs=(
            P("replica", "fsdp", None),
            P("replica", "fsdp", None),
            P("replica", "fsdp", None),
            P(),
            P("replica", "fsdp"),
            P(("replica", "fsdp"), None),
        ),
        out_specs=(
            P("replica", "fsdp", None),
            P("replica", "fsdp", None),
            P("replica", "fsdp", None),
        ),
        check_vma=False,
    )
```

```python
import functools

import jax
import jax.numpy as jnp
from jax import lax
from jax.experimental import pallas as pl
from jax.experimental.pallas import tpu as pltpu
from jax.sharding import PartitionSpec as P

CHUNKS = 8
LANE_CHUNKS = 32
DELAY = 4
GROUP = 8
ROW_TILE = 16
MIB = 1 << 20

decay_old = 0.5
grad_rate = 0.7
pull_rate = 0.9


def remote(src, dst, send_sem, recv_sem, **where):
    return pltpu.make_async_remote_copy(
        src_ref=src,
        dst_ref=dst,
        send_sem=send_sem,
        recv_sem=recv_sem,
        device_id=where,
        device_id_type=pl.DeviceIdType.MESH,
    )


def update(w, g, m, partner_w, partner_g):
    f32 = jnp.float32
    w, g = w.astype(f32), g.astype(f32)
    mean_w = (w + partner_w.astype(f32)) * 0.5
    mean_g = (g + partner_g.astype(f32)) * 0.5
    mom = decay_old * m.astype(f32) - grad_rate * mean_g - pull_rate * (w - mean_w)
    new_w = w + decay_old * mom - grad_rate * mean_g
    return new_w.astype(jnp.bfloat16), mom.astype(jnp.bfloat16)


def multiply(a_v, k_v, wg_v):
    feats = a_v.shape[1]
    step = 256 if feats % 256 == 0 else feats

    @pl.loop(0, feats // step)
    def _(t):
        cols = pl.ds(pl.multiple_of(t * step, step), step)
        wg_v[cols, :] = lax.dot_general(
            a_v[:, cols], k_v[...], (((0,), (0,)), ((), ())),
            preferred_element_type=jnp.float32).astype(wg_v.dtype)


def kernel(n, p, chunks, partner, weights, grad, momentum, acts, cotan,
           new_weights, new_momentum, weight_grad, *scratch):
    holds = scratch[:chunks]
    (routed, arrived, w_v, g_v, m_v, a_v, k_v, nw_v, nm_v, wg_v,
     spread_send, spread_recv, collect_send, collect_recv,
     k_send, k_recv, local_sem, self_sem, out_sem) = scratch[chunks:]
    me = lax.axis_index("replica")
    mz = lax.axis_index("fsdp")
    tok = cotan.shape[0]
    pieces = (weights, grad)

    barrier = pltpu.get_barrier_semaphore()

    @pl.loop(1, n)
    def _(d):
        pl.semaphore_signal(barrier, inc=1, device_id={"replica": lax.rem(me + d, n)},
                            device_id_type=pl.DeviceIdType.MESH)

    @pl.loop(1, p)
    def _(d):
        pl.semaphore_signal(barrier, inc=1, device_id={"fsdp": lax.rem(mz + d, p)},
                            device_id_type=pl.DeviceIdType.MESH)

    self_copies = []
    for c in range(chunks):
        for i in range(2):
            cp = pltpu.make_async_copy(pieces[i].at[me, c], holds[c].at[i, me], self_sem.at[c, i])
            cp.start()
            self_copies.append(cp)
    k_rows = pl.ds(pl.multiple_of(mz * tok, tok), tok)
    local_copies = [
        pltpu.make_async_copy(cotan, k_v.at[k_rows], local_sem.at[0]),
        pltpu.make_async_copy(weights, w_v, local_sem.at[1]),
        pltpu.make_async_copy(grad, g_v, local_sem.at[2]),
        pltpu.make_async_copy(momentum, m_v, local_sem.at[3]),
        pltpu.make_async_copy(acts, a_v, local_sem.at[4]),
    ]
    for cp in local_copies:
        cp.start()

    pl.semaphore_wait(barrier, n - 1 + p - 1)

    def spread(c, i, to):
        return remote(pieces[i].at[to, c], holds[c].at[i, me],
                      spread_send.at[c, i, to], spread_recv.at[c, i, me], replica=to)

    def spread_in(c, i, frm):
        return remote(pieces[i].at[frm, c], holds[c].at[i, frm],
                      spread_send.at[c, i, frm], spread_recv.at[c, i, frm], replica=frm)

    def collect(c, to):
        return remote(routed.at[c, to], arrived.at[c, me],
                      collect_send.at[c, to], collect_recv.at[c, me], replica=to)

    def collect_in(c, frm):
        return remote(routed.at[c, frm], arrived.at[c, frm],
                      collect_send.at[c, frm], collect_recv.at[c, frm], replica=frm)

    def share(to):
        return remote(cotan, k_v.at[k_rows], k_send.at[to], k_recv.at[mz], fsdp=to)

    def share_in(frm):
        rows = pl.ds(pl.multiple_of(frm * tok, tok), tok)
        return remote(cotan, k_v.at[rows], k_send.at[frm], k_recv.at[frm], fsdp=frm)

    for c in range(chunks):
        @pl.loop(1, n)
        def _(d, c=c):
            to = lax.rem(me + d, n)
            spread(c, 0, to).start()
            spread(c, 1, to).start()

        if c == 0:
            @pl.loop(1, p)
            def _(d):
                share(lax.rem(mz + d, p)).start()

    for c in range(chunks):
        self_copies[2 * c].wait()
        self_copies[2 * c + 1].wait()

        @pl.loop(1, n)
        def _(d, c=c):
            frm = lax.rem(me + n - d, n)
            spread_in(c, 0, frm).wait_recv()
            spread_in(c, 1, frm).wait_recv()

        @pl.loop(1, n)
        def _(d, c=c):
            to = lax.rem(me + d, n)
            source = partner[to]
            routed[c, to, 0] = holds[c][0, source]
            routed[c, to, 1] = holds[c][1, source]
            collect(c, to).start()

        source = partner[me]
        arrived[c, me, 0] = holds[c][0, source]
        arrived[c, me, 1] = holds[c][1, source]

    for cp in local_copies:
        cp.wait()

    @pl.loop(1, p)
    def _(d):
        share_in(lax.rem(mz + p - d, p)).wait_recv()

    multiply(a_v, k_v, wg_v)
    wg_out = pltpu.make_async_copy(wg_v, weight_grad, out_sem.at[2, 0])
    wg_out.start()

    out_copies = [wg_out]
    for c in range(chunks):
        @pl.loop(0, n)
        def _(d, c=c):
            frm = lax.rem(me + n - d, n)

            @pl.when(d > 0)
            def _():
                collect_in(c, frm).wait_recv()

            nw_v[frm, c], nm_v[frm, c] = update(
                w_v[frm, c], g_v[frm, c], m_v[frm, c], arrived[c, frm, 0], arrived[c, frm, 1])

        for i, (src, dst) in enumerate(((nw_v, new_weights), (nm_v, new_momentum))):
            cp = pltpu.make_async_copy(src.at[:, c], dst.at[:, c], out_sem.at[i, c])
            cp.start()
            out_copies.append(cp)

    for c in range(chunks):
        @pl.loop(1, n)
        def _(d, c=c):
            to = lax.rem(me + d, n)
            spread(c, 0, to).wait_send()
            spread(c, 1, to).wait_send()
            collect(c, to).wait_send()

    @pl.loop(1, p)
    def _(d):
        share(lax.rem(mz + d, p)).wait_send()

    for cp in out_copies:
        cp.wait()


def lane_kernel(p, chunks, groups, partner, weights, grad, momentum, acts, cotan,
                new_weights, new_momentum, weight_grad,
                own, rx, ry, tx, ty, handed, taken, w_v, g_v, m_v, a_v, k_v, nw_v, nm_v, wg_v,
                x_send, x_recv, y_send, y_recv, pair_send, pair_recv, hand_send, hand_recv,
                k_send, k_recv, local_sem, own_sem, out_sem):
    me = lax.axis_index("replica")
    mz = lax.axis_index("fsdp")
    core, chip = lax.rem(me, 2), lax.div(me, 2)
    x_chip = chip + 1 - 2 * lax.rem(chip, 2)
    y_chip = chip + 2 - 4 * lax.div(chip, 2)
    x_dev, y_dev, twin = 2 * x_chip + core, 2 * y_chip + core, 2 * chip + 1 - core
    tok = cotan.shape[0]
    pieces = (weights, grad)

    barrier = pltpu.get_barrier_semaphore()
    for peer in (x_dev, y_dev, twin):
        pl.semaphore_signal(barrier, inc=1, device_id={"replica": peer},
                            device_id_type=pl.DeviceIdType.MESH)

    @pl.loop(1, p)
    def _(d):
        pl.semaphore_signal(barrier, inc=1, device_id={"fsdp": lax.rem(mz + d, p)},
                            device_id_type=pl.DeviceIdType.MESH)

    def own_copy(j, i):
        at = pl.ds(groups[j][0], groups[j][1])
        return pltpu.make_async_copy(
            pieces[i].at[core, at], own.at[core, i, at], own_sem.at[j, i])

    for j in range(len(groups)):
        own_copy(j, 0).start()
        own_copy(j, 1).start()
    k_rows = pl.ds(pl.multiple_of(mz * tok, tok), tok)
    local_copies = [
        pltpu.make_async_copy(cotan, k_v.at[k_rows], local_sem.at[0]),
        pltpu.make_async_copy(weights, w_v, local_sem.at[1]),
        pltpu.make_async_copy(grad, g_v, local_sem.at[2]),
        pltpu.make_async_copy(momentum, m_v, local_sem.at[3]),
        pltpu.make_async_copy(acts, a_v, local_sem.at[4]),
    ]

    low, high = jnp.minimum(x_chip, y_chip), jnp.maximum(x_chip, y_chip)
    low_closed = partner[2 * low] == 2 * low + 1
    high_closed = partner[2 * high] == 2 * high + 1

    def route(i):
        j = partner[i]
        there = lax.div(j, 2)
        first = lax.rem(jnp.where(there < chip, j, i), 2)
        by_high = jnp.logical_and(high_closed,
                                  jnp.logical_or(jnp.logical_not(low_closed), first == 1))
        by = jnp.where(by_high, high, low)
        corner = jnp.where(by == x_chip, 3, 4)
        return jnp.where(there == chip, 0,
                         jnp.where(there == x_chip, 1, jnp.where(there == y_chip, 2, corner)))

    def starts_x(code):
        return jnp.logical_or(code == 1, code == 3)

    def starts_y(code):
        return jnp.logical_or(code == 2, code == 4)

    code0, code1 = route(2 * chip), route(2 * chip + 1)
    code_me, code_twin = route(me), route(twin)

    pl.semaphore_wait(barrier, 3 + p - 1)

    def pair(j, i):
        at = pl.ds(groups[j][0], groups[j][1])
        return remote(pieces[i].at[1 - core, at], own.at[core, i, at],
                      pair_send.at[j, i], pair_recv.at[j, i], replica=twin)

    def pair_in(j, i):
        at = pl.ds(groups[j][0], groups[j][1])
        return remote(pieces[i].at[1 - core, at], own.at[1 - core, i, at],
                      pair_send.at[j, i], pair_recv.at[j, i], replica=twin)

    def link_x(t):
        return remote(tx.at[t], rx.at[t], x_send.at[t], x_recv.at[t], replica=x_dev)

    def link_y(t):
        return remote(ty.at[t], ry.at[t], y_send.at[t], y_recv.at[t], replica=y_dev)

    def hand(c):
        return remote(handed.at[c], taken.at[c], hand_send.at[c], hand_recv.at[c], replica=twin)

    def share(to):
        return remote(cotan, k_v.at[k_rows], k_send.at[to], k_recv.at[mz], fsdp=to)

    def share_in(frm):
        rows = pl.ds(pl.multiple_of(frm * tok, tok), tok)
        return remote(cotan, k_v.at[rows], k_send.at[frm], k_recv.at[frm], fsdp=frm)

    for j in range(len(groups)):
        pair(j, 0).start()
        pair(j, 1).start()
        if j == 0:
            @pl.loop(1, p)
            def _(d):
                share(lax.rem(mz + d, p)).start()
    for cp in local_copies:
        cp.start()

    def pick(code, near, c):
        far = lax.select(code == 3, rx[c + DELAY], ry[c + DELAY])
        far = lax.select(code == 2, ry[c], far)
        far = lax.select(code == 1, rx[c], far)
        return lax.select(code == 0, near, far)

    out_copies = []

    def settle(half, c, got):
        nw_v[half, c], nm_v[half, c] = update(
            w_v[half, c], g_v[half, c], m_v[half, c], got[0], got[1])

    def finish(c):
        hand(c).wait_recv()
        settle(1 - core, c, taken[c])
        if c % GROUP == GROUP - 1:
            at = pl.ds(c - GROUP + 1, GROUP)
            for i, (src, dst) in enumerate(((nw_v, new_weights), (nm_v, new_momentum))):
                cp = pltpu.make_async_copy(src.at[:, at], dst.at[:, at], out_sem.at[i, c // GROUP])
                cp.start()
                out_copies.append(cp)

    def deliver(c):
        handed[c] = pick(code_twin, own[core, :, c], c)
        hand(c).start()
        settle(core, c, pick(code_me, own[1 - core, :, c], c))
        if c >= 2:
            finish(c - 2)

    for t in range(chunks + DELAY):
        for j, (at, _) in enumerate(groups):
            if at == t:
                for i in range(2):
                    own_copy(j, i).wait()
                    pair_in(j, i).wait_recv()
        if t < chunks:
            block0, block1 = own[0, :, t], own[1, :, t]
        if t >= DELAY:
            link_x(t - DELAY).wait_recv()
            link_y(t - DELAY).wait_recv()
            out_x, out_y = ry[t - DELAY], rx[t - DELAY]
        else:
            out_x, out_y = block1, block1
        if t < chunks:
            out_x = lax.select(starts_x(code0), block0, lax.select(starts_x(code1), block1, out_x))
            out_y = lax.select(starts_y(code0), block0, lax.select(starts_y(code1), block1, out_y))
        tx[t] = out_x
        link_x(t).start()
        ty[t] = out_y
        link_y(t).start()
        if t == 2 * DELAY:
            for cp in local_copies:
                cp.wait()
        if t >= 2 * DELAY:
            deliver(t - 2 * DELAY)

    @pl.loop(1, p)
    def _(d):
        share_in(lax.rem(mz + p - d, p)).wait_recv()

    multiply(a_v, k_v, wg_v)
    wg_out = pltpu.make_async_copy(wg_v, weight_grad, out_sem.at[2, 0])
    wg_out.start()
    out_copies.append(wg_out)

    for t in range(chunks, chunks + DELAY):
        link_x(t).wait_recv()
        link_y(t).wait_recv()
        deliver(t - DELAY)
    finish(chunks - 2)
    finish(chunks - 1)

    for t in range(chunks + DELAY):
        link_x(t).wait_send()
        link_y(t).wait_send()
    for c in range(chunks):
        hand(c).wait_send()
    for j in range(len(groups)):
        pair(j, 0).wait_send()
        pair(j, 1).wait_send()

    @pl.loop(1, p)
    def _(d):
        share(lax.rem(mz + d, p)).wait_send()

    for cp in out_copies:
        cp.wait()


def call(body, identity, view, operands, scratch):
    partner, weights, grad, momentum, acts, cotan = operands
    bf16 = jnp.bfloat16
    (tokens, feats), cols = acts.shape, cotan.shape[1]
    out_view = jax.ShapeDtypeStruct(view, bf16)
    any_space = pl.BlockSpec(memory_space=pl.ANY)
    return pl.pallas_call(
        body,
        out_shape=(out_view, out_view, jax.ShapeDtypeStruct((feats, cols), bf16)),
        in_specs=[pl.BlockSpec(memory_space=pltpu.SMEM)] + [any_space] * 5,
        out_specs=(any_space,) * 3,
        scratch_shapes=scratch,
        compiler_params=pltpu.CompilerParams(
            collective_id=identity, has_side_effects=True, vmem_limit_bytes=62 * MIB),
        cost_estimate=pl.CostEstimate(
            flops=2 * tokens * feats * cols, bytes_accessed=20 * weights.size // weights.shape[0],
            transcendentals=0),
    )(partner, weights.reshape(view), grad.reshape(view), momentum.reshape(view), acts, cotan)


def spread_form(n, p, weights, pseudo_grad, momentum, partner, activations, key_cotangent):
    rows, cols = weights.shape
    chunks = CHUNKS if rows >= n * CHUNKS * ROW_TILE else 1
    piece = -(-rows // (n * chunks * ROW_TILE)) * ROW_TILE
    padded = n * chunks * piece
    view = (n, chunks, piece, cols)

    def cut(x):
        return jnp.pad(x, ((0, padded - rows), (0, 0))) if padded != rows else x

    def join(x):
        return x.reshape(padded, cols)[:rows]

    bf16 = jnp.bfloat16
    tokens, feats = activations.shape
    dma = pltpu.SemaphoreType.DMA
    vmem = pltpu.VMEM
    scratch = [vmem((2, n, piece, cols), bf16) for _ in range(chunks)] + [
        vmem((chunks, n, 2, piece, cols), bf16), vmem((chunks, n, 2, piece, cols), bf16),
        vmem(view, bf16), vmem(view, bf16), vmem(view, bf16),
        vmem((tokens, feats), bf16), vmem((tokens, cols), bf16),
        vmem(view, bf16), vmem(view, bf16), vmem((feats, cols), bf16),
        dma((chunks, 2, n)), dma((chunks, 2, n)), dma((chunks, n)), dma((chunks, n)),
        dma((p,)), dma((p,)), dma((5,)), dma((chunks, 2)), dma((3, chunks)),
    ]
    new_weights, new_momentum, weight_grad = call(
        functools.partial(kernel, n, p, chunks), 0, view,
        (partner, cut(weights), cut(pseudo_grad), cut(momentum), activations, key_cotangent),
        scratch)
    return join(new_weights), join(new_momentum), weight_grad


def lane_form(p, weights, pseudo_grad, momentum, partner, activations, key_cotangent):
    rows, cols = weights.shape
    chunks = LANE_CHUNKS
    piece = rows // (2 * chunks)
    view = (2, chunks, piece, cols)
    groups = ((0, 2), (2, 2), (4, 4), (8, 8), (16, chunks - 16))
    bf16 = jnp.bfloat16
    tokens, feats = activations.shape
    dma = pltpu.SemaphoreType.DMA
    vmem = pltpu.VMEM
    lane = vmem((chunks + DELAY, 2, piece, cols), bf16)
    scratch = [
        vmem((2, 2, chunks, piece, cols), bf16), lane, lane, lane, lane,
        vmem((chunks, 2, piece, cols), bf16), vmem((chunks, 2, piece, cols), bf16),
        vmem(view, bf16), vmem(view, bf16), vmem(view, bf16),
        vmem((tokens, feats), bf16), vmem((tokens, cols), bf16),
        vmem(view, bf16), vmem(view, bf16), vmem((feats, cols), bf16),
        *[dma((chunks + DELAY,))] * 4,
        dma((len(groups), 2)), dma((len(groups), 2)), dma((chunks,)), dma((chunks,)),
        dma((p,)), dma((p,)), dma((5,)), dma((len(groups), 2)), dma((3, chunks // GROUP)),
    ]
    new_weights, new_momentum, weight_grad = call(
        functools.partial(lane_kernel, p, chunks, groups), 1, view,
        (partner, weights, pseudo_grad, momentum, activations, key_cotangent), scratch)
    return new_weights.reshape(rows, cols), new_momentum.reshape(rows, cols), weight_grad


def publish(arrays):
    parts = 2

    def body(*refs):
        sources, targets, sem = refs[:len(arrays)], refs[len(arrays):-1], refs[-1]
        copies = []
        for i, (source, target) in enumerate(zip(sources, targets)):
            size = source.shape[0] // parts
            for j in range(parts):
                at = pl.ds(j * size, size)
                copies.append(pltpu.make_async_copy(source.at[at], target.at[at], sem.at[i, j]))
        for cp in copies:
            cp.start()
        for cp in copies:
            cp.wait()

    any_space = pl.BlockSpec(memory_space=pl.ANY)
    total = sum(2 * x.size * x.dtype.itemsize for x in arrays)
    return pl.pallas_call(
        body,
        out_shape=tuple(jax.ShapeDtypeStruct(x.shape, x.dtype) for x in arrays),
        in_specs=[any_space] * len(arrays),
        out_specs=(any_space,) * len(arrays),
        scratch_shapes=[pltpu.SemaphoreType.DMA((len(arrays), parts))],
        cost_estimate=pl.CostEstimate(flops=0, bytes_accessed=total, transcendentals=0),
    )(*arrays)


def one_block_a_link(partner):
    index = lax.iota(jnp.int32, 8)
    over_x = (index // 2 + partner // 2) % 2
    over_y = (index // 4 + partner // 4) % 2
    crossings = jnp.sum(over_x + 16 * over_y)
    return (crossings == 0) | (crossings == 4 * 17)


def on_device(weights, pseudo_grad, momentum, partner, activations, key_cotangent):
    n, p = lax.axis_size("replica"), lax.axis_size("fsdp")
    operands = (weights[0], pseudo_grad[0], momentum[0], partner, activations, key_cotangent)
    spread = functools.partial(spread_form, n, p)
    if n == 8 and weights.shape[1] % (2 * LANE_CHUNKS * ROW_TILE) == 0:
        outs = lax.cond(one_block_a_link(partner), functools.partial(lane_form, p), spread,
                        *operands)
    else:
        outs = spread(*operands)
    return tuple(out[None] for out in publish(outs))


def solution(mesh):
    return jax.shard_map(
        on_device,
        mesh=mesh,
        in_specs=(
            P("replica", "fsdp", None),
            P("replica", "fsdp", None),
            P("replica", "fsdp", None),
            P(),
            P("replica", "fsdp"),
            P(("replica", "fsdp"), None),
        ),
        out_specs=(
            P("replica", "fsdp", None),
            P("replica", "fsdp", None),
            P("replica", "fsdp", None),
        ),
        check_vma=False,
    )
```

```python
import functools

import jax
import jax.numpy as jnp
from jax import lax
from jax.experimental import pallas as pl
from jax.experimental.pallas import tpu as pltpu
from jax.sharding import PartitionSpec as P

CHUNKS = 2
LANE_CHUNKS = 32
DELAY = 3
TILES = 4
GROUP = 8
ROW_TILE = 16
MIB = 1 << 20

decay_old = 0.5
grad_rate = 0.7
pull_rate = 0.9


def remote(src, dst, send_sem, recv_sem, **where):
    return pltpu.make_async_remote_copy(
        src_ref=src,
        dst_ref=dst,
        send_sem=send_sem,
        recv_sem=recv_sem,
        device_id=where,
        device_id_type=pl.DeviceIdType.MESH,
    )


def update(w, g, m, partner_w, partner_g):
    f32 = jnp.float32
    w, g = w.astype(f32), g.astype(f32)
    mean_w = (w + partner_w.astype(f32)) * 0.5
    mean_g = (g + partner_g.astype(f32)) * 0.5
    mom = decay_old * m.astype(f32) - grad_rate * mean_g - pull_rate * (w - mean_w)
    new_w = w + decay_old * mom - grad_rate * mean_g
    return new_w.astype(jnp.bfloat16), mom.astype(jnp.bfloat16)


def multiply(a_v, k_v, wg_v, tile):
    step = a_v.shape[1] // TILES
    cols = pl.ds(tile * step, step)
    wg_v[cols, :] = lax.dot_general(
        a_v[:, cols], k_v[...], (((0,), (0,)), ((), ())),
        preferred_element_type=jnp.float32).astype(wg_v.dtype)


def kernel(n, p, chunks, partner, weights, grad, momentum, acts, cotan,
           new_weights, new_momentum, weight_grad, *scratch):
    holds = scratch[:chunks]
    (routed, arrived, w_v, g_v, m_v, a_v, k_v, nw_v, nm_v, wg_v,
     spread_send, spread_recv, collect_send, collect_recv,
     k_send, k_recv, local_sem, self_sem, out_sem) = scratch[chunks:]
    me = lax.axis_index("replica")
    mz = lax.axis_index("fsdp")
    tok = cotan.shape[0]
    pieces = (weights, grad)

    barrier = pltpu.get_barrier_semaphore()

    @pl.loop(1, n)
    def _(d):
        pl.semaphore_signal(barrier, inc=1, device_id={"replica": lax.rem(me + d, n)},
                            device_id_type=pl.DeviceIdType.MESH)

    @pl.loop(1, p)
    def _(d):
        pl.semaphore_signal(barrier, inc=1, device_id={"fsdp": lax.rem(mz + d, p)},
                            device_id_type=pl.DeviceIdType.MESH)

    self_copies = []
    for c in range(chunks):
        for i in range(2):
            cp = pltpu.make_async_copy(pieces[i].at[me, c], holds[c].at[i, me], self_sem.at[c, i])
            cp.start()
            self_copies.append(cp)
    k_rows = pl.ds(pl.multiple_of(mz * tok, tok), tok)
    local_copies = [
        pltpu.make_async_copy(cotan, k_v.at[k_rows], local_sem.at[0]),
        pltpu.make_async_copy(weights, w_v, local_sem.at[1]),
        pltpu.make_async_copy(grad, g_v, local_sem.at[2]),
        pltpu.make_async_copy(momentum, m_v, local_sem.at[3]),
        pltpu.make_async_copy(acts, a_v, local_sem.at[4]),
    ]
    for cp in local_copies:
        cp.start()

    pl.semaphore_wait(barrier, n - 1 + p - 1)

    def spread(c, i, to):
        return remote(pieces[i].at[to, c], holds[c].at[i, me],
                      spread_send.at[c, i, to], spread_recv.at[c, i, me], replica=to)

    def spread_in(c, i, frm):
        return remote(pieces[i].at[frm, c], holds[c].at[i, frm],
                      spread_send.at[c, i, frm], spread_recv.at[c, i, frm], replica=frm)

    def collect(c, to):
        return remote(routed.at[c, to], arrived.at[c, me],
                      collect_send.at[c, to], collect_recv.at[c, me], replica=to)

    def collect_in(c, frm):
        return remote(routed.at[c, frm], arrived.at[c, frm],
                      collect_send.at[c, frm], collect_recv.at[c, frm], replica=frm)

    def share(to):
        return remote(cotan, k_v.at[k_rows], k_send.at[to], k_recv.at[mz], fsdp=to)

    def share_in(frm):
        rows = pl.ds(pl.multiple_of(frm * tok, tok), tok)
        return remote(cotan, k_v.at[rows], k_send.at[frm], k_recv.at[frm], fsdp=frm)

    for c in range(chunks):
        @pl.loop(1, n)
        def _(d, c=c):
            to = lax.rem(me + d, n)
            spread(c, 0, to).start()
            spread(c, 1, to).start()

        if c == 0:
            @pl.loop(1, p)
            def _(d):
                share(lax.rem(mz + d, p)).start()

    for c in range(chunks):
        self_copies[2 * c].wait()
        self_copies[2 * c + 1].wait()

        @pl.loop(1, n)
        def _(d, c=c):
            frm = lax.rem(me + n - d, n)
            spread_in(c, 0, frm).wait_recv()
            spread_in(c, 1, frm).wait_recv()

        @pl.loop(1, n)
        def _(d, c=c):
            to = lax.rem(me + d, n)
            source = partner[to]
            routed[c, to, 0] = holds[c][0, source]
            routed[c, to, 1] = holds[c][1, source]
            collect(c, to).start()

        source = partner[me]
        arrived[c, me, 0] = holds[c][0, source]
        arrived[c, me, 1] = holds[c][1, source]

    for cp in local_copies:
        cp.wait()

    @pl.loop(1, p)
    def _(d):
        share_in(lax.rem(mz + p - d, p)).wait_recv()

    for tile in range(TILES):
        multiply(a_v, k_v, wg_v, tile)

    wg_out = pltpu.make_async_copy(wg_v, weight_grad, out_sem.at[2, 0])
    wg_out.start()

    out_copies = [wg_out]
    for c in range(chunks):
        @pl.loop(0, n)
        def _(d, c=c):
            frm = lax.rem(me + n - d, n)

            @pl.when(d > 0)
            def _():
                collect_in(c, frm).wait_recv()

            nw_v[frm, c], nm_v[frm, c] = update(
                w_v[frm, c], g_v[frm, c], m_v[frm, c], arrived[c, frm, 0], arrived[c, frm, 1])

        for i, (src, dst) in enumerate(((nw_v, new_weights), (nm_v, new_momentum))):
            cp = pltpu.make_async_copy(src.at[:, c], dst.at[:, c], out_sem.at[i, c])
            cp.start()
            out_copies.append(cp)

    for c in range(chunks):
        @pl.loop(1, n)
        def _(d, c=c):
            to = lax.rem(me + d, n)
            spread(c, 0, to).wait_send()
            spread(c, 1, to).wait_send()
            collect(c, to).wait_send()

    @pl.loop(1, p)
    def _(d):
        share(lax.rem(mz + d, p)).wait_send()

    for cp in out_copies:
        cp.wait()


def lane_kernel(p, chunks, groups, partner, weights, grad, momentum, acts, cotan,
                new_weights, new_momentum, weight_grad,
                own, rx, ry, tx, ty, handed, taken, w_v, g_v, m_v, a_v, k_v, nw_v, nm_v, wg_v,
                x_send, x_recv, y_send, y_recv, pair_send, pair_recv, hand_send, hand_recv,
                k_send, k_recv, local_sem, own_sem, out_sem):
    me = lax.axis_index("replica")
    mz = lax.axis_index("fsdp")
    core, chip = lax.rem(me, 2), lax.div(me, 2)
    x_chip = chip + 1 - 2 * lax.rem(chip, 2)
    y_chip = chip + 2 - 4 * lax.div(chip, 2)
    x_dev, y_dev, twin = 2 * x_chip + core, 2 * y_chip + core, 2 * chip + 1 - core
    tok = cotan.shape[0]
    pieces = (weights, grad)

    barrier = pltpu.get_barrier_semaphore()
    for peer in (x_dev, y_dev, twin):
        pl.semaphore_signal(barrier, inc=1, device_id={"replica": peer},
                            device_id_type=pl.DeviceIdType.MESH)

    @pl.loop(1, p)
    def _(d):
        pl.semaphore_signal(barrier, inc=1, device_id={"fsdp": lax.rem(mz + d, p)},
                            device_id_type=pl.DeviceIdType.MESH)

    def own_copy(j, i):
        at = pl.ds(groups[j][0], groups[j][1])
        return pltpu.make_async_copy(
            pieces[i].at[core, at], own.at[core, i, at], own_sem.at[j, i])

    for j in range(len(groups)):
        own_copy(j, 0).start()
        own_copy(j, 1).start()
    k_rows = pl.ds(pl.multiple_of(mz * tok, tok), tok)
    local_copies = [
        pltpu.make_async_copy(cotan, k_v.at[k_rows], local_sem.at[0]),
        pltpu.make_async_copy(weights, w_v, local_sem.at[1]),
        pltpu.make_async_copy(grad, g_v, local_sem.at[2]),
        pltpu.make_async_copy(momentum, m_v, local_sem.at[3]),
        pltpu.make_async_copy(acts, a_v, local_sem.at[4]),
    ]

    low, high = jnp.minimum(x_chip, y_chip), jnp.maximum(x_chip, y_chip)
    low_closed = partner[2 * low] == 2 * low + 1
    high_closed = partner[2 * high] == 2 * high + 1

    def route(i):
        j = partner[i]
        there = lax.div(j, 2)
        first = lax.rem(jnp.where(there < chip, j, i), 2)
        by_high = jnp.logical_and(high_closed,
                                  jnp.logical_or(jnp.logical_not(low_closed), first == 1))
        by = jnp.where(by_high, high, low)
        corner = jnp.where(by == x_chip, 3, 4)
        return jnp.where(there == chip, 0,
                         jnp.where(there == x_chip, 1, jnp.where(there == y_chip, 2, corner)))

    def starts_x(code):
        return jnp.logical_or(code == 1, code == 3)

    def starts_y(code):
        return jnp.logical_or(code == 2, code == 4)

    code0, code1 = route(2 * chip), route(2 * chip + 1)
    code_me, code_twin = route(me), route(twin)

    pl.semaphore_wait(barrier, 3 + p - 1)

    def pair(j, i):
        at = pl.ds(groups[j][0], groups[j][1])
        return remote(pieces[i].at[1 - core, at], own.at[core, i, at],
                      pair_send.at[j, i], pair_recv.at[j, i], replica=twin)

    def pair_in(j, i):
        at = pl.ds(groups[j][0], groups[j][1])
        return remote(pieces[i].at[1 - core, at], own.at[1 - core, i, at],
                      pair_send.at[j, i], pair_recv.at[j, i], replica=twin)

    def link_x(t):
        return remote(tx.at[t], rx.at[t], x_send.at[t], x_recv.at[t], replica=x_dev)

    def link_y(t):
        return remote(ty.at[t], ry.at[t], y_send.at[t], y_recv.at[t], replica=y_dev)

    def hand(c):
        return remote(handed.at[c], taken.at[c], hand_send.at[c], hand_recv.at[c], replica=twin)

    def share(to):
        return remote(cotan, k_v.at[k_rows], k_send.at[to], k_recv.at[mz], fsdp=to)

    def share_in(frm):
        rows = pl.ds(pl.multiple_of(frm * tok, tok), tok)
        return remote(cotan, k_v.at[rows], k_send.at[frm], k_recv.at[frm], fsdp=frm)

    for j in range(len(groups)):
        pair(j, 0).start()
        pair(j, 1).start()
        if j == 0:
            @pl.loop(1, p)
            def _(d):
                share(lax.rem(mz + d, p)).start()
    for cp in local_copies:
        cp.start()

    def pick(code, near, c):
        far = lax.select(code == 3, rx[c + DELAY], ry[c + DELAY])
        far = lax.select(code == 2, ry[c], far)
        far = lax.select(code == 1, rx[c], far)
        return lax.select(code == 0, near, far)

    out_copies = []

    def settle(half, c, got):
        nw_v[half, c], nm_v[half, c] = update(
            w_v[half, c], g_v[half, c], m_v[half, c], got[0], got[1])

    def finish(c):
        hand(c).wait_recv()
        settle(1 - core, c, taken[c])
        if c % GROUP == GROUP - 1:
            at = pl.ds(c - GROUP + 1, GROUP)
            for i, (src, dst) in enumerate(((nw_v, new_weights), (nm_v, new_momentum))):
                cp = pltpu.make_async_copy(src.at[:, at], dst.at[:, at], out_sem.at[i, c // GROUP])
                cp.start()
                out_copies.append(cp)

    def deliver(c):
        handed[c] = pick(code_twin, own[core, :, c], c)
        hand(c).start()
        settle(core, c, pick(code_me, own[1 - core, :, c], c))
        if c >= 2:
            finish(c - 2)

    for t in range(chunks + DELAY):
        for j, (at, _) in enumerate(groups):
            if at == t:
                for i in range(2):
                    own_copy(j, i).wait()
                    pair_in(j, i).wait_recv()
        if t < chunks:
            block0, block1 = own[0, :, t], own[1, :, t]
        if t >= DELAY:
            link_x(t - DELAY).wait_recv()
            link_y(t - DELAY).wait_recv()
            out_x, out_y = ry[t - DELAY], rx[t - DELAY]
        else:
            out_x, out_y = block1, block1
        if t < chunks:
            out_x = lax.select(starts_x(code0), block0, lax.select(starts_x(code1), block1, out_x))
            out_y = lax.select(starts_y(code0), block0, lax.select(starts_y(code1), block1, out_y))
        tx[t] = out_x
        link_x(t).start()
        ty[t] = out_y
        link_y(t).start()
        if t == 2 * DELAY:
            for cp in local_copies:
                cp.wait()
        if t >= 2 * DELAY:
            deliver(t - 2 * DELAY)

    @pl.loop(1, p)
    def _(d):
        share_in(lax.rem(mz + p - d, p)).wait_recv()

    def tile_out(tile):
        multiply(a_v, k_v, wg_v, tile)
        step = a_v.shape[1] // TILES
        at = pl.ds(tile * step, step)
        cp = pltpu.make_async_copy(wg_v.at[at], weight_grad.at[at], out_sem.at[2, tile])
        cp.start()
        out_copies.append(cp)

    tile_out(0)
    tile_out(1)
    for t in range(chunks, chunks + DELAY):
        link_x(t).wait_recv()
        link_y(t).wait_recv()
        deliver(t - DELAY)
        if t < chunks + 2:
            tile_out(2 + t - chunks)
    finish(chunks - 2)
    finish(chunks - 1)

    for t in range(chunks + DELAY):
        link_x(t).wait_send()
        link_y(t).wait_send()
    for c in range(chunks):
        hand(c).wait_send()
    for j in range(len(groups)):
        pair(j, 0).wait_send()
        pair(j, 1).wait_send()

    @pl.loop(1, p)
    def _(d):
        share(lax.rem(mz + d, p)).wait_send()

    for cp in out_copies:
        cp.wait()


def call(body, identity, view, operands, scratch):
    partner, weights, grad, momentum, acts, cotan = operands
    bf16 = jnp.bfloat16
    (tokens, feats), cols = acts.shape, cotan.shape[1]
    out_view = jax.ShapeDtypeStruct(view, bf16)
    any_space = pl.BlockSpec(memory_space=pl.ANY)
    return pl.pallas_call(
        body,
        out_shape=(out_view, out_view, jax.ShapeDtypeStruct((feats, cols), bf16)),
        in_specs=[pl.BlockSpec(memory_space=pltpu.SMEM)] + [any_space] * 5,
        out_specs=(any_space,) * 3,
        scratch_shapes=scratch,
        compiler_params=pltpu.CompilerParams(
            collective_id=identity, has_side_effects=True, vmem_limit_bytes=62 * MIB),
        cost_estimate=pl.CostEstimate(
            flops=2 * tokens * feats * cols, bytes_accessed=20 * weights.size // weights.shape[0],
            transcendentals=0),
    )(partner, weights.reshape(view), grad.reshape(view), momentum.reshape(view), acts, cotan)


def spread_form(n, p, weights, pseudo_grad, momentum, partner, activations, key_cotangent):
    rows, cols = weights.shape
    chunks = CHUNKS if rows >= n * CHUNKS * ROW_TILE else 1
    piece = -(-rows // (n * chunks * ROW_TILE)) * ROW_TILE
    padded = n * chunks * piece
    view = (n, chunks, piece, cols)

    def cut(x):
        return jnp.pad(x, ((0, padded - rows), (0, 0))) if padded != rows else x

    def join(x):
        return x.reshape(padded, cols)[:rows]

    bf16 = jnp.bfloat16
    tokens, feats = activations.shape
    dma = pltpu.SemaphoreType.DMA
    vmem = pltpu.VMEM
    scratch = [vmem((2, n, piece, cols), bf16) for _ in range(chunks)] + [
        vmem((chunks, n, 2, piece, cols), bf16), vmem((chunks, n, 2, piece, cols), bf16),
        vmem(view, bf16), vmem(view, bf16), vmem(view, bf16),
        vmem((tokens, feats), bf16), vmem((tokens, cols), bf16),
        vmem(view, bf16), vmem(view, bf16), vmem((feats, cols), bf16),
        dma((chunks, 2, n)), dma((chunks, 2, n)), dma((chunks, n)), dma((chunks, n)),
        dma((p,)), dma((p,)), dma((5,)), dma((chunks, 2)), dma((3, chunks)),
    ]
    new_weights, new_momentum, weight_grad = call(
        functools.partial(kernel, n, p, chunks), 0, view,
        (partner, cut(weights), cut(pseudo_grad), cut(momentum), activations, key_cotangent),
        scratch)
    return join(new_weights), join(new_momentum), weight_grad


def lane_form(p, weights, pseudo_grad, momentum, partner, activations, key_cotangent):
    rows, cols = weights.shape
    chunks = LANE_CHUNKS
    piece = rows // (2 * chunks)
    view = (2, chunks, piece, cols)
    groups = ((0, 2), (2, 2), (4, 4), (8, 8), (16, chunks - 16))
    bf16 = jnp.bfloat16
    tokens, feats = activations.shape
    dma = pltpu.SemaphoreType.DMA
    vmem = pltpu.VMEM
    lane = vmem((chunks + DELAY, 2, piece, cols), bf16)
    scratch = [
        vmem((2, 2, chunks, piece, cols), bf16), lane, lane, lane, lane,
        vmem((chunks, 2, piece, cols), bf16), vmem((chunks, 2, piece, cols), bf16),
        vmem(view, bf16), vmem(view, bf16), vmem(view, bf16),
        vmem((tokens, feats), bf16), vmem((tokens, cols), bf16),
        vmem(view, bf16), vmem(view, bf16), vmem((feats, cols), bf16),
        *[dma((chunks + DELAY,))] * 4,
        dma((len(groups), 2)), dma((len(groups), 2)), dma((chunks,)), dma((chunks,)),
        dma((p,)), dma((p,)), dma((5,)), dma((len(groups), 2)), dma((3, chunks // GROUP)),
    ]
    new_weights, new_momentum, weight_grad = call(
        functools.partial(lane_kernel, p, chunks, groups), 1, view,
        (partner, weights, pseudo_grad, momentum, activations, key_cotangent), scratch)
    return new_weights.reshape(rows, cols), new_momentum.reshape(rows, cols), weight_grad


def publish(arrays):
    parts = 2
    count = len(arrays)

    def body(*refs):
        sources, targets, held = refs[:count], refs[count:2 * count], refs[2 * count:3 * count]
        in_sem, out_sem = refs[3 * count:]

        def copy(i, j, first, second, sem):
            size = first[i].shape[0] // parts
            at = pl.ds(j * size, size)
            return pltpu.make_async_copy(first[i].at[at], second[i].at[at], sem.at[i, j])

        each = [(i, j) for i in range(count) for j in range(parts)]
        for i, j in each:
            copy(i, j, sources, held, in_sem).start()
        for i, j in each:
            copy(i, j, sources, held, in_sem).wait()
            copy(i, j, held, targets, out_sem).start()
        for i, j in each:
            copy(i, j, held, targets, out_sem).wait()

    any_space = pl.BlockSpec(memory_space=pl.ANY)
    total = sum(2 * x.size * x.dtype.itemsize for x in arrays)
    return pl.pallas_call(
        body,
        out_shape=tuple(jax.ShapeDtypeStruct(x.shape, x.dtype) for x in arrays),
        in_specs=[any_space] * len(arrays),
        out_specs=(any_space,) * len(arrays),
        scratch_shapes=[pltpu.VMEM(x.shape, x.dtype) for x in arrays]
        + [pltpu.SemaphoreType.DMA((count, parts))] * 2,
        compiler_params=pltpu.CompilerParams(vmem_limit_bytes=16 * MIB),
        cost_estimate=pl.CostEstimate(flops=0, bytes_accessed=total, transcendentals=0),
    )(*arrays)


def one_block_a_link(partner):
    index = lax.iota(jnp.int32, 8)
    over_x = (index // 2 + partner // 2) % 2
    over_y = (index // 4 + partner // 4) % 2
    crossings = jnp.sum(over_x + 16 * over_y)
    return (crossings == 0) | (crossings == 4 * 17)


def on_device(weights, pseudo_grad, momentum, partner, activations, key_cotangent):
    n, p = lax.axis_size("replica"), lax.axis_size("fsdp")
    operands = (weights[0], pseudo_grad[0], momentum[0], partner, activations, key_cotangent)
    spread = functools.partial(spread_form, n, p)
    if n == 8 and weights.shape[1] % (2 * LANE_CHUNKS * ROW_TILE) == 0:
        outs = lax.cond(one_block_a_link(partner), functools.partial(lane_form, p), spread,
                        *operands)
    else:
        outs = spread(*operands)
    return tuple(out[None] for out in publish(outs))


def solution(mesh):
    return jax.shard_map(
        on_device,
        mesh=mesh,
        in_specs=(
            P("replica", "fsdp", None),
            P("replica", "fsdp", None),
            P("replica", "fsdp", None),
            P(),
            P("replica", "fsdp"),
            P(("replica", "fsdp"), None),
        ),
        out_specs=(
            P("replica", "fsdp", None),
            P("replica", "fsdp", None),
            P("replica", "fsdp", None),
        ),
        check_vma=False,
    )
```

```python
import functools

import jax
import jax.numpy as jnp
from jax import lax
from jax.experimental import pallas as pl
from jax.experimental.pallas import tpu as pltpu
from jax.sharding import PartitionSpec as P

CHUNKS = 2
LANE_CHUNKS = 32
DELAY = 5
TILES = 4
GROUP = 8
ROW_TILE = 16
MIB = 1 << 20

decay_old = 0.5
grad_rate = 0.7
pull_rate = 0.9


def remote(src, dst, send_sem, recv_sem, **where):
    return pltpu.make_async_remote_copy(
        src_ref=src,
        dst_ref=dst,
        send_sem=send_sem,
        recv_sem=recv_sem,
        device_id=where,
        device_id_type=pl.DeviceIdType.MESH,
    )


def update(w, g, m, partner_w, partner_g):
    f32 = jnp.float32
    w, g = w.astype(f32), g.astype(f32)
    mean_w = (w + partner_w.astype(f32)) * 0.5
    mean_g = (g + partner_g.astype(f32)) * 0.5
    mom = decay_old * m.astype(f32) - grad_rate * mean_g - pull_rate * (w - mean_w)
    new_w = w + decay_old * mom - grad_rate * mean_g
    return new_w.astype(jnp.bfloat16), mom.astype(jnp.bfloat16)


def multiply(a_v, k_v, wg_v, tile):
    step = a_v.shape[1] // TILES
    cols = pl.ds(tile * step, step)
    wg_v[cols, :] = lax.dot_general(
        a_v[:, cols], k_v[...], (((0,), (0,)), ((), ())),
        preferred_element_type=jnp.float32).astype(wg_v.dtype)


def kernel(n, p, chunks, partner, weights, grad, momentum, acts, cotan,
           new_weights, new_momentum, weight_grad, *scratch):
    holds = scratch[:chunks]
    (routed, arrived, w_v, g_v, m_v, a_v, k_v, nw_v, nm_v, wg_v,
     spread_send, spread_recv, collect_send, collect_recv,
     k_send, k_recv, local_sem, self_sem, out_sem) = scratch[chunks:]
    me = lax.axis_index("replica")
    mz = lax.axis_index("fsdp")
    tok = cotan.shape[0]
    pieces = (weights, grad)

    barrier = pltpu.get_barrier_semaphore()

    @pl.loop(1, n)
    def _(d):
        pl.semaphore_signal(barrier, inc=1, device_id={"replica": lax.rem(me + d, n)},
                            device_id_type=pl.DeviceIdType.MESH)

    @pl.loop(1, p)
    def _(d):
        pl.semaphore_signal(barrier, inc=1, device_id={"fsdp": lax.rem(mz + d, p)},
                            device_id_type=pl.DeviceIdType.MESH)

    self_copies = []
    for c in range(chunks):
        for i in range(2):
            cp = pltpu.make_async_copy(pieces[i].at[me, c], holds[c].at[i, me], self_sem.at[c, i])
            cp.start()
            self_copies.append(cp)
    k_rows = pl.ds(pl.multiple_of(mz * tok, tok), tok)
    local_copies = [
        pltpu.make_async_copy(cotan, k_v.at[k_rows], local_sem.at[0]),
        pltpu.make_async_copy(weights, w_v, local_sem.at[1]),
        pltpu.make_async_copy(grad, g_v, local_sem.at[2]),
        pltpu.make_async_copy(momentum, m_v, local_sem.at[3]),
        pltpu.make_async_copy(acts, a_v, local_sem.at[4]),
    ]
    for cp in local_copies:
        cp.start()

    pl.semaphore_wait(barrier, n - 1 + p - 1)

    def spread(c, i, to):
        return remote(pieces[i].at[to, c], holds[c].at[i, me],
                      spread_send.at[c, i, to], spread_recv.at[c, i, me], replica=to)

    def spread_in(c, i, frm):
        return remote(pieces[i].at[frm, c], holds[c].at[i, frm],
                      spread_send.at[c, i, frm], spread_recv.at[c, i, frm], replica=frm)

    def collect(c, to):
        return remote(routed.at[c, to], arrived.at[c, me],
                      collect_send.at[c, to], collect_recv.at[c, me], replica=to)

    def collect_in(c, frm):
        return remote(routed.at[c, frm], arrived.at[c, frm],
                      collect_send.at[c, frm], collect_recv.at[c, frm], replica=frm)

    def share(to):
        return remote(cotan, k_v.at[k_rows], k_send.at[to], k_recv.at[mz], fsdp=to)

    def share_in(frm):
        rows = pl.ds(pl.multiple_of(frm * tok, tok), tok)
        return remote(cotan, k_v.at[rows], k_send.at[frm], k_recv.at[frm], fsdp=frm)

    for c in range(chunks):
        @pl.loop(1, n)
        def _(d, c=c):
            to = lax.rem(me + d, n)
            spread(c, 0, to).start()
            spread(c, 1, to).start()

        if c == 0:
            @pl.loop(1, p)
            def _(d):
                share(lax.rem(mz + d, p)).start()

    for c in range(chunks):
        self_copies[2 * c].wait()
        self_copies[2 * c + 1].wait()

        @pl.loop(1, n)
        def _(d, c=c):
            frm = lax.rem(me + n - d, n)
            spread_in(c, 0, frm).wait_recv()
            spread_in(c, 1, frm).wait_recv()

        @pl.loop(1, n)
        def _(d, c=c):
            to = lax.rem(me + d, n)
            source = partner[to]
            routed[c, to, 0] = holds[c][0, source]
            routed[c, to, 1] = holds[c][1, source]
            collect(c, to).start()

        source = partner[me]
        arrived[c, me, 0] = holds[c][0, source]
        arrived[c, me, 1] = holds[c][1, source]

    for cp in local_copies:
        cp.wait()

    @pl.loop(1, p)
    def _(d):
        share_in(lax.rem(mz + p - d, p)).wait_recv()

    for tile in range(TILES):
        multiply(a_v, k_v, wg_v, tile)

    wg_out = pltpu.make_async_copy(wg_v, weight_grad, out_sem.at[2, 0])
    wg_out.start()

    out_copies = [wg_out]
    for c in range(chunks):
        @pl.loop(0, n)
        def _(d, c=c):
            frm = lax.rem(me + n - d, n)

            @pl.when(d > 0)
            def _():
                collect_in(c, frm).wait_recv()

            nw_v[frm, c], nm_v[frm, c] = update(
                w_v[frm, c], g_v[frm, c], m_v[frm, c], arrived[c, frm, 0], arrived[c, frm, 1])

        for i, (src, dst) in enumerate(((nw_v, new_weights), (nm_v, new_momentum))):
            cp = pltpu.make_async_copy(src.at[:, c], dst.at[:, c], out_sem.at[i, c])
            cp.start()
            out_copies.append(cp)

    for c in range(chunks):
        @pl.loop(1, n)
        def _(d, c=c):
            to = lax.rem(me + d, n)
            spread(c, 0, to).wait_send()
            spread(c, 1, to).wait_send()
            collect(c, to).wait_send()

    @pl.loop(1, p)
    def _(d):
        share(lax.rem(mz + d, p)).wait_send()

    for cp in out_copies:
        cp.wait()


def lane_kernel(p, chunks, groups, partner, weights, grad, momentum, acts, cotan,
                new_weights, new_momentum, weight_grad,
                own, rx, ry, tx, ty, handed, taken, w_v, g_v, m_v, a_v, k_v, nw_v, nm_v, wg_v,
                x_send, x_recv, y_send, y_recv, pair_send, pair_recv, hand_send, hand_recv,
                k_send, k_recv, local_sem, own_sem, out_sem):
    me = lax.axis_index("replica")
    mz = lax.axis_index("fsdp")
    core, chip = lax.rem(me, 2), lax.div(me, 2)
    x_chip = chip + 1 - 2 * lax.rem(chip, 2)
    y_chip = chip + 2 - 4 * lax.div(chip, 2)
    x_dev, y_dev, twin = 2 * x_chip + core, 2 * y_chip + core, 2 * chip + 1 - core
    tok = cotan.shape[0]
    pieces = (weights, grad)

    barrier = pltpu.get_barrier_semaphore()
    for peer in (x_dev, y_dev, twin):
        pl.semaphore_signal(barrier, inc=1, device_id={"replica": peer},
                            device_id_type=pl.DeviceIdType.MESH)

    @pl.loop(1, p)
    def _(d):
        pl.semaphore_signal(barrier, inc=1, device_id={"fsdp": lax.rem(mz + d, p)},
                            device_id_type=pl.DeviceIdType.MESH)

    def own_copy(j, i):
        at = pl.ds(groups[j][0], groups[j][1])
        return pltpu.make_async_copy(
            pieces[i].at[core, at], own.at[core, i, at], own_sem.at[j, i])

    for j in range(len(groups)):
        own_copy(j, 0).start()
        own_copy(j, 1).start()
    k_rows = pl.ds(pl.multiple_of(mz * tok, tok), tok)
    local_copies = [
        pltpu.make_async_copy(cotan, k_v.at[k_rows], local_sem.at[0]),
        pltpu.make_async_copy(weights, w_v, local_sem.at[1]),
        pltpu.make_async_copy(grad, g_v, local_sem.at[2]),
        pltpu.make_async_copy(momentum, m_v, local_sem.at[3]),
        pltpu.make_async_copy(acts, a_v, local_sem.at[4]),
    ]

    low, high = jnp.minimum(x_chip, y_chip), jnp.maximum(x_chip, y_chip)
    low_closed = partner[2 * low] == 2 * low + 1
    high_closed = partner[2 * high] == 2 * high + 1

    def route(i):
        j = partner[i]
        there = lax.div(j, 2)
        first = lax.rem(jnp.where(there < chip, j, i), 2)
        by_high = jnp.logical_and(high_closed,
                                  jnp.logical_or(jnp.logical_not(low_closed), first == 1))
        by = jnp.where(by_high, high, low)
        corner = jnp.where(by == x_chip, 3, 4)
        return jnp.where(there == chip, 0,
                         jnp.where(there == x_chip, 1, jnp.where(there == y_chip, 2, corner)))

    def starts_x(code):
        return jnp.logical_or(code == 1, code == 3)

    def starts_y(code):
        return jnp.logical_or(code == 2, code == 4)

    code0, code1 = route(2 * chip), route(2 * chip + 1)
    code_me, code_twin = route(me), route(twin)

    pl.semaphore_wait(barrier, 3 + p - 1)

    def pair(j, i):
        at = pl.ds(groups[j][0], groups[j][1])
        return remote(pieces[i].at[1 - core, at], own.at[core, i, at],
                      pair_send.at[j, i], pair_recv.at[j, i], replica=twin)

    def pair_in(j, i):
        at = pl.ds(groups[j][0], groups[j][1])
        return remote(pieces[i].at[1 - core, at], own.at[1 - core, i, at],
                      pair_send.at[j, i], pair_recv.at[j, i], replica=twin)

    def link_x(t):
        return remote(tx.at[t], rx.at[t], x_send.at[t], x_recv.at[t], replica=x_dev)

    def link_y(t):
        return remote(ty.at[t], ry.at[t], y_send.at[t], y_recv.at[t], replica=y_dev)

    def hand(c):
        return remote(handed.at[c], taken.at[c], hand_send.at[c], hand_recv.at[c], replica=twin)

    def share(to):
        return remote(cotan, k_v.at[k_rows], k_send.at[to], k_recv.at[mz], fsdp=to)

    def share_in(frm):
        rows = pl.ds(pl.multiple_of(frm * tok, tok), tok)
        return remote(cotan, k_v.at[rows], k_send.at[frm], k_recv.at[frm], fsdp=frm)

    for j in range(len(groups)):
        pair(j, 0).start()
        pair(j, 1).start()
        if j == 0:
            @pl.loop(1, p)
            def _(d):
                share(lax.rem(mz + d, p)).start()
    for cp in local_copies:
        cp.start()

    def pick(code, near, c):
        far = lax.select(code == 3, rx[c + DELAY], ry[c + DELAY])
        far = lax.select(code == 2, ry[c], far)
        far = lax.select(code == 1, rx[c], far)
        return lax.select(code == 0, near, far)

    out_copies = []

    def settle(half, c, got):
        nw_v[half, c], nm_v[half, c] = update(
            w_v[half, c], g_v[half, c], m_v[half, c], got[0], got[1])

    def finish(c):
        hand(c).wait_recv()
        settle(1 - core, c, taken[c])
        if c % GROUP == GROUP - 1:
            at = pl.ds(c - GROUP + 1, GROUP)
            for i, (src, dst) in enumerate(((nw_v, new_weights), (nm_v, new_momentum))):
                cp = pltpu.make_async_copy(src.at[:, at], dst.at[:, at], out_sem.at[i, c // GROUP])
                cp.start()
                out_copies.append(cp)

    def deliver(c):
        handed[c] = pick(code_twin, own[core, :, c], c)
        hand(c).start()
        settle(core, c, pick(code_me, own[1 - core, :, c], c))
        if c >= 2:
            finish(c - 2)

    for t in range(chunks + DELAY):
        for j, (at, _) in enumerate(groups):
            if at == t:
                for i in range(2):
                    own_copy(j, i).wait()
                    pair_in(j, i).wait_recv()
        if t < chunks:
            block0, block1 = own[0, :, t], own[1, :, t]
        if t >= DELAY:
            link_x(t - DELAY).wait_recv()
            link_y(t - DELAY).wait_recv()
            out_x, out_y = ry[t - DELAY], rx[t - DELAY]
        else:
            out_x, out_y = block1, block1
        if t < chunks:
            out_x = lax.select(starts_x(code0), block0, lax.select(starts_x(code1), block1, out_x))
            out_y = lax.select(starts_y(code0), block0, lax.select(starts_y(code1), block1, out_y))
        tx[t] = out_x
        link_x(t).start()
        ty[t] = out_y
        link_y(t).start()
        if t == 2 * DELAY:
            for cp in local_copies:
                cp.wait()
        if t >= 2 * DELAY:
            deliver(t - 2 * DELAY)

    @pl.loop(1, p)
    def _(d):
        share_in(lax.rem(mz + p - d, p)).wait_recv()

    def tile_out(tile):
        multiply(a_v, k_v, wg_v, tile)
        step = a_v.shape[1] // TILES
        at = pl.ds(tile * step, step)
        cp = pltpu.make_async_copy(wg_v.at[at], weight_grad.at[at], out_sem.at[2, tile])
        cp.start()
        out_copies.append(cp)

    tile_out(0)
    tile_out(1)
    for t in range(chunks, chunks + DELAY):
        link_x(t).wait_recv()
        link_y(t).wait_recv()
        deliver(t - DELAY)
        if t < chunks + 2:
            tile_out(2 + t - chunks)
    finish(chunks - 2)
    finish(chunks - 1)

    for t in range(chunks + DELAY):
        link_x(t).wait_send()
        link_y(t).wait_send()
    for c in range(chunks):
        hand(c).wait_send()
    for j in range(len(groups)):
        pair(j, 0).wait_send()
        pair(j, 1).wait_send()

    @pl.loop(1, p)
    def _(d):
        share(lax.rem(mz + d, p)).wait_send()

    for cp in out_copies:
        cp.wait()


def call(body, identity, view, operands, scratch):
    partner, weights, grad, momentum, acts, cotan = operands
    bf16 = jnp.bfloat16
    (tokens, feats), cols = acts.shape, cotan.shape[1]
    out_view = jax.ShapeDtypeStruct(view, bf16)
    any_space = pl.BlockSpec(memory_space=pl.ANY)
    return pl.pallas_call(
        body,
        out_shape=(out_view, out_view, jax.ShapeDtypeStruct((feats, cols), bf16)),
        in_specs=[pl.BlockSpec(memory_space=pltpu.SMEM)]
        + [pl.BlockSpec(memory_space=pltpu.HBM)] * 5,
        out_specs=(any_space,) * 3,
        scratch_shapes=scratch,
        compiler_params=pltpu.CompilerParams(
            collective_id=identity, has_side_effects=True, vmem_limit_bytes=32 * MIB),
        cost_estimate=pl.CostEstimate(
            flops=2 * tokens * feats * cols, bytes_accessed=20 * weights.size // weights.shape[0],
            transcendentals=0),
    )(partner, weights.reshape(view), grad.reshape(view), momentum.reshape(view), acts, cotan)


def spread_form(n, p, weights, pseudo_grad, momentum, partner, activations, key_cotangent):
    rows, cols = weights.shape
    chunks = CHUNKS if rows >= n * CHUNKS * ROW_TILE else 1
    piece = -(-rows // (n * chunks * ROW_TILE)) * ROW_TILE
    padded = n * chunks * piece
    view = (n, chunks, piece, cols)

    def cut(x):
        return jnp.pad(x, ((0, padded - rows), (0, 0))) if padded != rows else x

    def join(x):
        return x.reshape(padded, cols)[:rows]

    bf16 = jnp.bfloat16
    tokens, feats = activations.shape
    dma = pltpu.SemaphoreType.DMA
    vmem = pltpu.VMEM
    scratch = [vmem((2, n, piece, cols), bf16) for _ in range(chunks)] + [
        vmem((chunks, n, 2, piece, cols), bf16), vmem((chunks, n, 2, piece, cols), bf16),
        vmem(view, bf16), vmem(view, bf16), vmem(view, bf16),
        vmem((tokens, feats), bf16), vmem((tokens, cols), bf16),
        vmem(view, bf16), vmem(view, bf16), vmem((feats, cols), bf16),
        dma((chunks, 2, n)), dma((chunks, 2, n)), dma((chunks, n)), dma((chunks, n)),
        dma((p,)), dma((p,)), dma((5,)), dma((chunks, 2)), dma((3, chunks)),
    ]
    new_weights, new_momentum, weight_grad = call(
        functools.partial(kernel, n, p, chunks), 0, view,
        (partner, cut(weights), cut(pseudo_grad), cut(momentum), activations, key_cotangent),
        scratch)
    return join(new_weights), join(new_momentum), weight_grad


def lane_form(p, weights, pseudo_grad, momentum, partner, activations, key_cotangent):
    rows, cols = weights.shape
    chunks = LANE_CHUNKS
    piece = rows // (2 * chunks)
    view = (2, chunks, piece, cols)
    groups = ((0, 2), (2, 2), (4, 4), (8, 8), (16, chunks - 16))
    bf16 = jnp.bfloat16
    tokens, feats = activations.shape
    dma = pltpu.SemaphoreType.DMA
    vmem = pltpu.VMEM
    lane = vmem((chunks + DELAY, 2, piece, cols), bf16)
    scratch = [
        vmem((2, 2, chunks, piece, cols), bf16), lane, lane, lane, lane,
        vmem((chunks, 2, piece, cols), bf16), vmem((chunks, 2, piece, cols), bf16),
        vmem(view, bf16), vmem(view, bf16), vmem(view, bf16),
        vmem((tokens, feats), bf16), vmem((tokens, cols), bf16),
        vmem(view, bf16), vmem(view, bf16), vmem((feats, cols), bf16),
        *[dma((chunks + DELAY,))] * 4,
        dma((len(groups), 2)), dma((len(groups), 2)), dma((chunks,)), dma((chunks,)),
        dma((p,)), dma((p,)), dma((5,)), dma((len(groups), 2)), dma((3, chunks // GROUP)),
    ]
    new_weights, new_momentum, weight_grad = call(
        functools.partial(lane_kernel, p, chunks, groups), 1, view,
        (partner, weights, pseudo_grad, momentum, activations, key_cotangent), scratch)
    return new_weights.reshape(rows, cols), new_momentum.reshape(rows, cols), weight_grad


def publish(arrays):
    parts = 2
    count = len(arrays)

    def body(*refs):
        sources, targets, held = refs[:count], refs[count:2 * count], refs[2 * count:3 * count]
        in_sem, out_sem = refs[3 * count:]

        def copy(i, j, first, second, sem):
            size = first[i].shape[0] // parts
            at = pl.ds(j * size, size)
            return pltpu.make_async_copy(first[i].at[at], second[i].at[at], sem.at[i, j])

        each = [(i, j) for i in range(count) for j in range(parts)]
        for i, j in each:
            copy(i, j, sources, held, in_sem).start()
        for i, j in each:
            copy(i, j, sources, held, in_sem).wait()
            copy(i, j, held, targets, out_sem).start()
        for i, j in each:
            copy(i, j, held, targets, out_sem).wait()

    any_space = pl.BlockSpec(memory_space=pl.ANY)
    total = sum(2 * x.size * x.dtype.itemsize for x in arrays)
    return pl.pallas_call(
        body,
        out_shape=tuple(jax.ShapeDtypeStruct(x.shape, x.dtype) for x in arrays),
        in_specs=[any_space] * len(arrays),
        out_specs=(any_space,) * len(arrays),
        scratch_shapes=[pltpu.VMEM(x.shape, x.dtype) for x in arrays]
        + [pltpu.SemaphoreType.DMA((count, parts))] * 2,
        compiler_params=pltpu.CompilerParams(vmem_limit_bytes=16 * MIB),
        cost_estimate=pl.CostEstimate(flops=0, bytes_accessed=total, transcendentals=0),
    )(*arrays)


def one_block_a_link(partner):
    index = lax.iota(jnp.int32, 8)
    over_x = (index // 2 + partner // 2) % 2
    over_y = (index // 4 + partner // 4) % 2
    crossings = jnp.sum(over_x + 16 * over_y)
    return (crossings == 0) | (crossings == 4 * 17)


def on_device(weights, pseudo_grad, momentum, partner, activations, key_cotangent):
    n, p = lax.axis_size("replica"), lax.axis_size("fsdp")
    operands = (weights[0], pseudo_grad[0], momentum[0], partner, activations, key_cotangent)
    spread = functools.partial(spread_form, n, p)
    if n == 8 and weights.shape[1] % (2 * LANE_CHUNKS * ROW_TILE) == 0:
        outs = lax.cond(one_block_a_link(partner), functools.partial(lane_form, p), spread,
                        *operands)
    else:
        outs = spread(*operands)
    return tuple(out[None] for out in publish(outs))


def solution(mesh):
    return jax.shard_map(
        on_device,
        mesh=mesh,
        in_specs=(
            P("replica", "fsdp", None),
            P("replica", "fsdp", None),
            P("replica", "fsdp", None),
            P(),
            P("replica", "fsdp"),
            P(("replica", "fsdp"), None),
        ),
        out_specs=(
            P("replica", "fsdp", None),
            P("replica", "fsdp", None),
            P("replica", "fsdp", None),
        ),
        check_vma=False,
    )
```

```python
import functools

import jax
import jax.numpy as jnp
from jax import lax
from jax.experimental import pallas as pl
from jax.experimental.pallas import tpu as pltpu
from jax.sharding import PartitionSpec as P

CHUNKS = 2
LANE_CHUNKS = 32
DELAY = 5
TILES = 4
GROUP = 8
ROW_TILE = 16
MIB = 1 << 20

decay_old = 0.5
grad_rate = 0.7
pull_rate = 0.9


def remote(src, dst, send_sem, recv_sem, **where):
    return pltpu.make_async_remote_copy(
        src_ref=src,
        dst_ref=dst,
        send_sem=send_sem,
        recv_sem=recv_sem,
        device_id=where,
        device_id_type=pl.DeviceIdType.MESH,
    )


def update(w, g, m, partner_w, partner_g):
    f32 = jnp.float32
    w, g = w.astype(f32), g.astype(f32)
    mean_w = (w + partner_w.astype(f32)) * 0.5
    mean_g = (g + partner_g.astype(f32)) * 0.5
    mom = decay_old * m.astype(f32) - grad_rate * mean_g - pull_rate * (w - mean_w)
    new_w = w + decay_old * mom - grad_rate * mean_g
    return new_w.astype(jnp.bfloat16), mom.astype(jnp.bfloat16)


def multiply(a_v, k_v, wg_v, tile):
    step = a_v.shape[1] // TILES
    cols = pl.ds(tile * step, step)
    wg_v[cols, :] = lax.dot_general(
        a_v[:, cols], k_v[...], (((0,), (0,)), ((), ())),
        preferred_element_type=jnp.float32).astype(wg_v.dtype)


def kernel(n, p, chunks, partner, weights, grad, momentum, acts, cotan,
           new_weights, new_momentum, weight_grad, *scratch):
    holds = scratch[:chunks]
    (routed, arrived, w_v, g_v, m_v, a_v, k_v, nw_v, nm_v, wg_v,
     spread_send, spread_recv, collect_send, collect_recv,
     k_send, k_recv, local_sem, self_sem, out_sem) = scratch[chunks:]
    me = lax.axis_index("replica")
    mz = lax.axis_index("fsdp")
    tok = cotan.shape[0]
    pieces = (weights, grad)

    barrier = pltpu.get_barrier_semaphore()

    @pl.loop(1, n)
    def _(d):
        pl.semaphore_signal(barrier, inc=1, device_id={"replica": lax.rem(me + d, n)},
                            device_id_type=pl.DeviceIdType.MESH)

    @pl.loop(1, p)
    def _(d):
        pl.semaphore_signal(barrier, inc=1, device_id={"fsdp": lax.rem(mz + d, p)},
                            device_id_type=pl.DeviceIdType.MESH)

    self_copies = []
    for c in range(chunks):
        for i in range(2):
            cp = pltpu.make_async_copy(pieces[i].at[me, c], holds[c].at[i, me], self_sem.at[c, i])
            cp.start()
            self_copies.append(cp)
    k_rows = pl.ds(pl.multiple_of(mz * tok, tok), tok)
    local_copies = [
        pltpu.make_async_copy(cotan, k_v.at[k_rows], local_sem.at[0]),
        pltpu.make_async_copy(weights, w_v, local_sem.at[1]),
        pltpu.make_async_copy(grad, g_v, local_sem.at[2]),
        pltpu.make_async_copy(momentum, m_v, local_sem.at[3]),
        pltpu.make_async_copy(acts, a_v, local_sem.at[4]),
    ]
    for cp in local_copies:
        cp.start()

    pl.semaphore_wait(barrier, n - 1 + p - 1)

    def spread(c, i, to):
        return remote(pieces[i].at[to, c], holds[c].at[i, me],
                      spread_send.at[c, i, to], spread_recv.at[c, i, me], replica=to)

    def spread_in(c, i, frm):
        return remote(pieces[i].at[frm, c], holds[c].at[i, frm],
                      spread_send.at[c, i, frm], spread_recv.at[c, i, frm], replica=frm)

    def collect(c, to):
        return remote(routed.at[c, to], arrived.at[c, me],
                      collect_send.at[c, to], collect_recv.at[c, me], replica=to)

    def collect_in(c, frm):
        return remote(routed.at[c, frm], arrived.at[c, frm],
                      collect_send.at[c, frm], collect_recv.at[c, frm], replica=frm)

    def share(to):
        return remote(cotan, k_v.at[k_rows], k_send.at[to], k_recv.at[mz], fsdp=to)

    def share_in(frm):
        rows = pl.ds(pl.multiple_of(frm * tok, tok), tok)
        return remote(cotan, k_v.at[rows], k_send.at[frm], k_recv.at[frm], fsdp=frm)

    for c in range(chunks):
        @pl.loop(1, n)
        def _(d, c=c):
            to = lax.rem(me + d, n)
            spread(c, 0, to).start()
            spread(c, 1, to).start()

        if c == 0:
            @pl.loop(1, p)
            def _(d):
                share(lax.rem(mz + d, p)).start()

    for c in range(chunks):
        self_copies[2 * c].wait()
        self_copies[2 * c + 1].wait()

        @pl.loop(1, n)
        def _(d, c=c):
            frm = lax.rem(me + n - d, n)
            spread_in(c, 0, frm).wait_recv()
            spread_in(c, 1, frm).wait_recv()

        @pl.loop(1, n)
        def _(d, c=c):
            to = lax.rem(me + d, n)
            source = partner[to]
            routed[c, to, 0] = holds[c][0, source]
            routed[c, to, 1] = holds[c][1, source]
            collect(c, to).start()

        source = partner[me]
        arrived[c, me, 0] = holds[c][0, source]
        arrived[c, me, 1] = holds[c][1, source]

    for cp in local_copies:
        cp.wait()

    @pl.loop(1, p)
    def _(d):
        share_in(lax.rem(mz + p - d, p)).wait_recv()

    for tile in range(TILES):
        multiply(a_v, k_v, wg_v, tile)

    wg_out = pltpu.make_async_copy(wg_v, weight_grad, out_sem.at[2, 0])
    wg_out.start()

    out_copies = [wg_out]
    for c in range(chunks):
        @pl.loop(0, n)
        def _(d, c=c):
            frm = lax.rem(me + n - d, n)

            @pl.when(d > 0)
            def _():
                collect_in(c, frm).wait_recv()

            nw_v[frm, c], nm_v[frm, c] = update(
                w_v[frm, c], g_v[frm, c], m_v[frm, c], arrived[c, frm, 0], arrived[c, frm, 1])

        for i, (src, dst) in enumerate(((nw_v, new_weights), (nm_v, new_momentum))):
            cp = pltpu.make_async_copy(src.at[:, c], dst.at[:, c], out_sem.at[i, c])
            cp.start()
            out_copies.append(cp)

    for c in range(chunks):
        @pl.loop(1, n)
        def _(d, c=c):
            to = lax.rem(me + d, n)
            spread(c, 0, to).wait_send()
            spread(c, 1, to).wait_send()
            collect(c, to).wait_send()

    @pl.loop(1, p)
    def _(d):
        share(lax.rem(mz + d, p)).wait_send()

    for cp in out_copies:
        cp.wait()


def lane_kernel(p, chunks, groups, partner, weights, grad, momentum, acts, cotan,
                new_weights, new_momentum, weight_grad,
                own, rx, ry, tx, ty, handed, taken, w_v, g_v, m_v, a_v, k_v, nw_v, nm_v, wg_v,
                x_send, x_recv, y_send, y_recv, pair_send, pair_recv, hand_send, hand_recv,
                k_send, k_recv, local_sem, own_sem, out_sem):
    me = lax.axis_index("replica")
    mz = lax.axis_index("fsdp")
    core, chip = lax.rem(me, 2), lax.div(me, 2)
    x_chip = chip + 1 - 2 * lax.rem(chip, 2)
    y_chip = chip + 2 - 4 * lax.div(chip, 2)
    x_dev, y_dev, twin = 2 * x_chip + core, 2 * y_chip + core, 2 * chip + 1 - core
    tok = cotan.shape[0]
    pieces = (weights, grad)

    barrier = pltpu.get_barrier_semaphore()
    for peer in (x_dev, y_dev, twin):
        pl.semaphore_signal(barrier, inc=1, device_id={"replica": peer},
                            device_id_type=pl.DeviceIdType.MESH)

    @pl.loop(1, p)
    def _(d):
        pl.semaphore_signal(barrier, inc=1, device_id={"fsdp": lax.rem(mz + d, p)},
                            device_id_type=pl.DeviceIdType.MESH)

    def own_copy(j, i):
        at = pl.ds(groups[j][0], groups[j][1])
        return pltpu.make_async_copy(
            pieces[i].at[core, at], own.at[core, i, at], own_sem.at[j, i])

    for j in range(len(groups)):
        own_copy(j, 0).start()
        own_copy(j, 1).start()
    k_rows = pl.ds(pl.multiple_of(mz * tok, tok), tok)
    local_copies = [
        pltpu.make_async_copy(cotan, k_v.at[k_rows], local_sem.at[0]),
        pltpu.make_async_copy(weights, w_v, local_sem.at[1]),
        pltpu.make_async_copy(grad, g_v, local_sem.at[2]),
        pltpu.make_async_copy(momentum, m_v, local_sem.at[3]),
        pltpu.make_async_copy(acts, a_v, local_sem.at[4]),
    ]

    low, high = jnp.minimum(x_chip, y_chip), jnp.maximum(x_chip, y_chip)
    low_closed = partner[2 * low] == 2 * low + 1
    high_closed = partner[2 * high] == 2 * high + 1

    def route(i):
        j = partner[i]
        there = lax.div(j, 2)
        first = lax.rem(jnp.where(there < chip, j, i), 2)
        by_high = jnp.logical_and(high_closed,
                                  jnp.logical_or(jnp.logical_not(low_closed), first == 1))
        by = jnp.where(by_high, high, low)
        corner = jnp.where(by == x_chip, 3, 4)
        return jnp.where(there == chip, 0,
                         jnp.where(there == x_chip, 1, jnp.where(there == y_chip, 2, corner)))

    def starts_x(code):
        return jnp.logical_or(code == 1, code == 3)

    def starts_y(code):
        return jnp.logical_or(code == 2, code == 4)

    code0, code1 = route(2 * chip), route(2 * chip + 1)
    code_me, code_twin = route(me), route(twin)

    pl.semaphore_wait(barrier, 3 + p - 1)

    def pair(j, i):
        at = pl.ds(groups[j][0], groups[j][1])
        return remote(pieces[i].at[1 - core, at], own.at[core, i, at],
                      pair_send.at[j, i], pair_recv.at[j, i], replica=twin)

    def pair_in(j, i):
        at = pl.ds(groups[j][0], groups[j][1])
        return remote(pieces[i].at[1 - core, at], own.at[1 - core, i, at],
                      pair_send.at[j, i], pair_recv.at[j, i], replica=twin)

    def link_x(t):
        return remote(tx.at[t], rx.at[t], x_send.at[t], x_recv.at[t], replica=x_dev)

    def link_y(t):
        return remote(ty.at[t], ry.at[t], y_send.at[t], y_recv.at[t], replica=y_dev)

    def hand(c):
        return remote(handed.at[c], taken.at[c], hand_send.at[c], hand_recv.at[c], replica=twin)

    def share(to):
        return remote(cotan, k_v.at[k_rows], k_send.at[to], k_recv.at[mz], fsdp=to)

    def share_in(frm):
        rows = pl.ds(pl.multiple_of(frm * tok, tok), tok)
        return remote(cotan, k_v.at[rows], k_send.at[frm], k_recv.at[frm], fsdp=frm)

    for j in range(len(groups)):
        pair(j, 0).start()
        pair(j, 1).start()
        if j == 0:
            @pl.loop(1, p)
            def _(d):
                share(lax.rem(mz + d, p)).start()

    def pick(code, near, c):
        far = lax.select(code == 3, rx[c + DELAY], ry[c + DELAY])
        far = lax.select(code == 2, ry[c], far)
        far = lax.select(code == 1, rx[c], far)
        return lax.select(code == 0, near, far)

    out_copies = []

    def settle(half, c, got):
        nw_v[half, c], nm_v[half, c] = update(
            w_v[half, c], g_v[half, c], m_v[half, c], got[0], got[1])

    def finish(c):
        hand(c).wait_recv()
        settle(1 - core, c, taken[c])
        if c % GROUP == GROUP - 1:
            at = pl.ds(c - GROUP + 1, GROUP)
            for i, (src, dst) in enumerate(((nw_v, new_weights), (nm_v, new_momentum))):
                cp = pltpu.make_async_copy(src.at[:, at], dst.at[:, at], out_sem.at[i, c // GROUP])
                cp.start()
                out_copies.append(cp)

    def deliver(c):
        handed[c] = pick(code_twin, own[core, :, c], c)
        hand(c).start()
        settle(core, c, pick(code_me, own[1 - core, :, c], c))
        if c >= 2:
            finish(c - 2)

    for t in range(chunks + DELAY):
        for j, (at, _) in enumerate(groups):
            if at == t:
                for i in range(2):
                    own_copy(j, i).wait()
                    pair_in(j, i).wait_recv()
        if t < chunks:
            block0, block1 = own[0, :, t], own[1, :, t]
        if t >= DELAY:
            link_x(t - DELAY).wait_recv()
            link_y(t - DELAY).wait_recv()
            out_x, out_y = ry[t - DELAY], rx[t - DELAY]
        else:
            out_x, out_y = block1, block1
        if t < chunks:
            out_x = lax.select(starts_x(code0), block0, lax.select(starts_x(code1), block1, out_x))
            out_y = lax.select(starts_y(code0), block0, lax.select(starts_y(code1), block1, out_y))
        tx[t] = out_x
        link_x(t).start()
        ty[t] = out_y
        link_y(t).start()
        if t == 1:
            for cp in local_copies:
                cp.start()
        if t == 2 * DELAY:
            for cp in local_copies:
                cp.wait()
        if t >= 2 * DELAY:
            deliver(t - 2 * DELAY)

    @pl.loop(1, p)
    def _(d):
        share_in(lax.rem(mz + p - d, p)).wait_recv()

    def tile_out(tile):
        multiply(a_v, k_v, wg_v, tile)
        step = a_v.shape[1] // TILES
        at = pl.ds(tile * step, step)
        cp = pltpu.make_async_copy(wg_v.at[at], weight_grad.at[at], out_sem.at[2, tile])
        cp.start()
        out_copies.append(cp)

    tile_out(0)
    tile_out(1)
    for t in range(chunks, chunks + DELAY):
        link_x(t).wait_recv()
        link_y(t).wait_recv()
        deliver(t - DELAY)
        if t < chunks + 2:
            tile_out(2 + t - chunks)
    finish(chunks - 2)
    finish(chunks - 1)

    for t in range(chunks + DELAY):
        link_x(t).wait_send()
        link_y(t).wait_send()
    for c in range(chunks):
        hand(c).wait_send()
    for j in range(len(groups)):
        pair(j, 0).wait_send()
        pair(j, 1).wait_send()

    @pl.loop(1, p)
    def _(d):
        share(lax.rem(mz + d, p)).wait_send()

    for cp in out_copies:
        cp.wait()


def call(body, identity, view, operands, scratch):
    partner, weights, grad, momentum, acts, cotan = operands
    bf16 = jnp.bfloat16
    (tokens, feats), cols = acts.shape, cotan.shape[1]
    out_view = jax.ShapeDtypeStruct(view, bf16)
    any_space = pl.BlockSpec(memory_space=pl.ANY)
    return pl.pallas_call(
        body,
        out_shape=(out_view, out_view, jax.ShapeDtypeStruct((feats, cols), bf16)),
        in_specs=[pl.BlockSpec(memory_space=pltpu.SMEM)]
        + [pl.BlockSpec(memory_space=pltpu.HBM)] * 5,
        out_specs=(any_space,) * 3,
        scratch_shapes=scratch,
        compiler_params=pltpu.CompilerParams(
            collective_id=identity, has_side_effects=True, vmem_limit_bytes=32 * MIB),
        cost_estimate=pl.CostEstimate(
            flops=2 * tokens * feats * cols, bytes_accessed=20 * weights.size // weights.shape[0],
            transcendentals=0),
    )(partner, weights.reshape(view), grad.reshape(view), momentum.reshape(view), acts, cotan)


def spread_form(n, p, weights, pseudo_grad, momentum, partner, activations, key_cotangent):
    rows, cols = weights.shape
    chunks = CHUNKS if rows >= n * CHUNKS * ROW_TILE else 1
    piece = -(-rows // (n * chunks * ROW_TILE)) * ROW_TILE
    padded = n * chunks * piece
    view = (n, chunks, piece, cols)

    def cut(x):
        return jnp.pad(x, ((0, padded - rows), (0, 0))) if padded != rows else x

    def join(x):
        return x.reshape(padded, cols)[:rows]

    bf16 = jnp.bfloat16
    tokens, feats = activations.shape
    dma = pltpu.SemaphoreType.DMA
    vmem = pltpu.VMEM
    scratch = [vmem((2, n, piece, cols), bf16) for _ in range(chunks)] + [
        vmem((chunks, n, 2, piece, cols), bf16), vmem((chunks, n, 2, piece, cols), bf16),
        vmem(view, bf16), vmem(view, bf16), vmem(view, bf16),
        vmem((tokens, feats), bf16), vmem((tokens, cols), bf16),
        vmem(view, bf16), vmem(view, bf16), vmem((feats, cols), bf16),
        dma((chunks, 2, n)), dma((chunks, 2, n)), dma((chunks, n)), dma((chunks, n)),
        dma((p,)), dma((p,)), dma((5,)), dma((chunks, 2)), dma((3, chunks)),
    ]
    new_weights, new_momentum, weight_grad = call(
        functools.partial(kernel, n, p, chunks), 0, view,
        (partner, cut(weights), cut(pseudo_grad), cut(momentum), activations, key_cotangent),
        scratch)
    return join(new_weights), join(new_momentum), weight_grad


def lane_form(p, weights, pseudo_grad, momentum, partner, activations, key_cotangent):
    rows, cols = weights.shape
    chunks = LANE_CHUNKS
    piece = rows // (2 * chunks)
    view = (2, chunks, piece, cols)
    groups = ((0, 2), (2, 2), (4, 4), (8, 8), (16, chunks - 16))
    bf16 = jnp.bfloat16
    tokens, feats = activations.shape
    dma = pltpu.SemaphoreType.DMA
    vmem = pltpu.VMEM
    lane = vmem((chunks + DELAY, 2, piece, cols), bf16)
    scratch = [
        vmem((2, 2, chunks, piece, cols), bf16), lane, lane, lane, lane,
        vmem((chunks, 2, piece, cols), bf16), vmem((chunks, 2, piece, cols), bf16),
        vmem(view, bf16), vmem(view, bf16), vmem(view, bf16),
        vmem((tokens, feats), bf16), vmem((tokens, cols), bf16),
        vmem(view, bf16), vmem(view, bf16), vmem((feats, cols), bf16),
        *[dma((chunks + DELAY,))] * 4,
        dma((len(groups), 2)), dma((len(groups), 2)), dma((chunks,)), dma((chunks,)),
        dma((p,)), dma((p,)), dma((5,)), dma((len(groups), 2)), dma((3, chunks // GROUP)),
    ]
    new_weights, new_momentum, weight_grad = call(
        functools.partial(lane_kernel, p, chunks, groups), 1, view,
        (partner, weights, pseudo_grad, momentum, activations, key_cotangent), scratch)
    return new_weights.reshape(rows, cols), new_momentum.reshape(rows, cols), weight_grad


def publish(arrays):
    parts = 2
    count = len(arrays)

    def body(*refs):
        sources, targets, sem = refs[:count], refs[count:2 * count], refs[-1]
        copies = []
        for i, (source, target) in enumerate(zip(sources, targets)):
            size = source.shape[0] // parts
            for j in range(parts):
                at = pl.ds(j * size, size)
                copies.append(pltpu.make_async_copy(source.at[at], target.at[at], sem.at[i, j]))
        for cp in copies:
            cp.start()
        for cp in copies:
            cp.wait()

    any_space = pl.BlockSpec(memory_space=pl.ANY)
    total = sum(2 * x.size * x.dtype.itemsize for x in arrays)
    return pl.pallas_call(
        body,
        out_shape=tuple(jax.ShapeDtypeStruct(x.shape, x.dtype) for x in arrays),
        in_specs=[pl.BlockSpec(memory_space=pltpu.VMEM)] * count,
        out_specs=(any_space,) * count,
        scratch_shapes=[pltpu.SemaphoreType.DMA((count, parts))],
        compiler_params=pltpu.CompilerParams(vmem_limit_bytes=16 * MIB),
        cost_estimate=pl.CostEstimate(flops=0, bytes_accessed=total, transcendentals=0),
    )(*arrays)


def one_block_a_link(partner):
    index = lax.iota(jnp.int32, 8)
    over_x = (index // 2 + partner // 2) % 2
    over_y = (index // 4 + partner // 4) % 2
    crossings = jnp.sum(over_x + 16 * over_y)
    return (crossings == 0) | (crossings == 4 * 17)


def on_device(weights, pseudo_grad, momentum, partner, activations, key_cotangent):
    n, p = lax.axis_size("replica"), lax.axis_size("fsdp")
    operands = (weights[0], pseudo_grad[0], momentum[0], partner, activations, key_cotangent)
    spread = functools.partial(spread_form, n, p)
    if n == 8 and weights.shape[1] % (2 * LANE_CHUNKS * ROW_TILE) == 0:
        outs = lax.cond(one_block_a_link(partner), functools.partial(lane_form, p), spread,
                        *operands)
    else:
        outs = spread(*operands)
    return tuple(out[None] for out in publish(outs))


def solution(mesh):
    return jax.shard_map(
        on_device,
        mesh=mesh,
        in_specs=(
            P("replica", "fsdp", None),
            P("replica", "fsdp", None),
            P("replica", "fsdp", None),
            P(),
            P("replica", "fsdp"),
            P(("replica", "fsdp"), None),
        ),
        out_specs=(
            P("replica", "fsdp", None),
            P("replica", "fsdp", None),
            P("replica", "fsdp", None),
        ),
        check_vma=False,
    )
```

```python
import functools

import jax
import jax.numpy as jnp
from jax import lax
from jax.experimental import pallas as pl
from jax.experimental.pallas import tpu as pltpu
from jax.sharding import PartitionSpec as P

CHUNKS = 2
LANE_CHUNKS = 32
DELAY = 5
LAG = 5
TILES = 4
GROUP = 8
ROW_TILE = 16
MIB = 1 << 20

decay_old = 0.5
grad_rate = 0.7
pull_rate = 0.9


def remote(src, dst, send_sem, recv_sem, **where):
    return pltpu.make_async_remote_copy(
        src_ref=src,
        dst_ref=dst,
        send_sem=send_sem,
        recv_sem=recv_sem,
        device_id=where,
        device_id_type=pl.DeviceIdType.MESH,
    )


def update(w, g, m, partner_w, partner_g):
    f32 = jnp.float32
    w, g = w.astype(f32), g.astype(f32)
    mean_w = (w + partner_w.astype(f32)) * 0.5
    mean_g = (g + partner_g.astype(f32)) * 0.5
    mom = decay_old * m.astype(f32) - grad_rate * mean_g - pull_rate * (w - mean_w)
    new_w = w + decay_old * mom - grad_rate * mean_g
    return new_w.astype(jnp.bfloat16), mom.astype(jnp.bfloat16)


def multiply(a_v, k_v, wg_v, tile):
    step = a_v.shape[1] // TILES
    cols = pl.ds(tile * step, step)
    wg_v[cols, :] = lax.dot_general(
        a_v[:, cols], k_v[...], (((0,), (0,)), ((), ())),
        preferred_element_type=jnp.float32).astype(wg_v.dtype)


def kernel(n, p, chunks, partner, weights, grad, momentum, acts, cotan,
           new_weights, new_momentum, weight_grad, *scratch):
    holds = scratch[:chunks]
    (routed, arrived, w_v, g_v, m_v, a_v, k_v, nw_v, nm_v, wg_v,
     spread_send, spread_recv, collect_send, collect_recv,
     k_send, k_recv, local_sem, self_sem, out_sem) = scratch[chunks:]
    me = lax.axis_index("replica")
    mz = lax.axis_index("fsdp")
    tok = cotan.shape[0]
    pieces = (weights, grad)

    barrier = pltpu.get_barrier_semaphore()

    @pl.loop(1, n)
    def _(d):
        pl.semaphore_signal(barrier, inc=1, device_id={"replica": lax.rem(me + d, n)},
                            device_id_type=pl.DeviceIdType.MESH)

    @pl.loop(1, p)
    def _(d):
        pl.semaphore_signal(barrier, inc=1, device_id={"fsdp": lax.rem(mz + d, p)},
                            device_id_type=pl.DeviceIdType.MESH)

    self_copies = []
    for c in range(chunks):
        for i in range(2):
            cp = pltpu.make_async_copy(pieces[i].at[me, c], holds[c].at[i, me], self_sem.at[c, i])
            cp.start()
            self_copies.append(cp)
    k_rows = pl.ds(pl.multiple_of(mz * tok, tok), tok)
    local_copies = [
        pltpu.make_async_copy(cotan, k_v.at[k_rows], local_sem.at[0]),
        pltpu.make_async_copy(weights, w_v, local_sem.at[1]),
        pltpu.make_async_copy(grad, g_v, local_sem.at[2]),
        pltpu.make_async_copy(momentum, m_v, local_sem.at[3]),
        pltpu.make_async_copy(acts, a_v, local_sem.at[4]),
    ]
    pl.semaphore_wait(barrier, n - 1 + p - 1)

    def spread(c, i, to):
        return remote(pieces[i].at[to, c], holds[c].at[i, me],
                      spread_send.at[c, i, to], spread_recv.at[c, i, me], replica=to)

    def spread_in(c, i, frm):
        return remote(pieces[i].at[frm, c], holds[c].at[i, frm],
                      spread_send.at[c, i, frm], spread_recv.at[c, i, frm], replica=frm)

    def collect(c, to):
        return remote(routed.at[c, to], arrived.at[c, me],
                      collect_send.at[c, to], collect_recv.at[c, me], replica=to)

    def collect_in(c, frm):
        return remote(routed.at[c, frm], arrived.at[c, frm],
                      collect_send.at[c, frm], collect_recv.at[c, frm], replica=frm)

    def share(to):
        return remote(cotan, k_v.at[k_rows], k_send.at[to], k_recv.at[mz], fsdp=to)

    def share_in(frm):
        rows = pl.ds(pl.multiple_of(frm * tok, tok), tok)
        return remote(cotan, k_v.at[rows], k_send.at[frm], k_recv.at[frm], fsdp=frm)

    for c in range(chunks):
        @pl.loop(1, n)
        def _(d, c=c):
            to = lax.rem(me + d, n)
            spread(c, 0, to).start()
            spread(c, 1, to).start()

        if c == 0:
            @pl.loop(1, p)
            def _(d):
                share(lax.rem(mz + d, p)).start()

    for cp in local_copies:
        cp.start()

    for c in range(chunks):
        self_copies[2 * c].wait()
        self_copies[2 * c + 1].wait()

        @pl.loop(1, n)
        def _(d, c=c):
            frm = lax.rem(me + n - d, n)
            spread_in(c, 0, frm).wait_recv()
            spread_in(c, 1, frm).wait_recv()

        @pl.loop(1, n)
        def _(d, c=c):
            to = lax.rem(me + d, n)
            source = partner[to]
            routed[c, to, 0] = holds[c][0, source]
            routed[c, to, 1] = holds[c][1, source]
            collect(c, to).start()

        source = partner[me]
        arrived[c, me, 0] = holds[c][0, source]
        arrived[c, me, 1] = holds[c][1, source]

    for cp in local_copies:
        cp.wait()

    @pl.loop(1, p)
    def _(d):
        share_in(lax.rem(mz + p - d, p)).wait_recv()

    for tile in range(TILES):
        multiply(a_v, k_v, wg_v, tile)

    wg_out = pltpu.make_async_copy(wg_v, weight_grad, out_sem.at[2, 0])
    wg_out.start()

    out_copies = [wg_out]
    for c in range(chunks):
        @pl.loop(0, n)
        def _(d, c=c):
            frm = lax.rem(me + n - d, n)

            @pl.when(d > 0)
            def _():
                collect_in(c, frm).wait_recv()

            nw_v[frm, c], nm_v[frm, c] = update(
                w_v[frm, c], g_v[frm, c], m_v[frm, c], arrived[c, frm, 0], arrived[c, frm, 1])

        for i, (src, dst) in enumerate(((nw_v, new_weights), (nm_v, new_momentum))):
            cp = pltpu.make_async_copy(src.at[:, c], dst.at[:, c], out_sem.at[i, c])
            cp.start()
            out_copies.append(cp)

    for c in range(chunks):
        @pl.loop(1, n)
        def _(d, c=c):
            to = lax.rem(me + d, n)
            spread(c, 0, to).wait_send()
            spread(c, 1, to).wait_send()
            collect(c, to).wait_send()

    @pl.loop(1, p)
    def _(d):
        share(lax.rem(mz + d, p)).wait_send()

    for cp in out_copies:
        cp.wait()


def lane_kernel(p, chunks, groups, partner, weights, grad, momentum, acts, cotan,
                new_weights, new_momentum, weight_grad,
                own, rx, ry, tx, ty, handed, taken, w_v, g_v, m_v, a_v, k_v, nw_v, nm_v, wg_v,
                x_send, x_recv, y_send, y_recv, pair_send, pair_recv, hand_send, hand_recv,
                k_send, k_recv, local_sem, own_sem, out_sem):
    me = lax.axis_index("replica")
    mz = lax.axis_index("fsdp")
    core, chip = lax.rem(me, 2), lax.div(me, 2)
    x_chip = chip + 1 - 2 * lax.rem(chip, 2)
    y_chip = chip + 2 - 4 * lax.div(chip, 2)
    x_dev, y_dev, twin = 2 * x_chip + core, 2 * y_chip + core, 2 * chip + 1 - core
    tok = cotan.shape[0]
    pieces = (weights, grad)

    barrier = pltpu.get_barrier_semaphore()
    for peer in (x_dev, y_dev, twin):
        pl.semaphore_signal(barrier, inc=1, device_id={"replica": peer},
                            device_id_type=pl.DeviceIdType.MESH)

    @pl.loop(1, p)
    def _(d):
        pl.semaphore_signal(barrier, inc=1, device_id={"fsdp": lax.rem(mz + d, p)},
                            device_id_type=pl.DeviceIdType.MESH)

    def own_copy(j, i):
        at = pl.ds(groups[j][0], groups[j][1])
        return pltpu.make_async_copy(
            pieces[i].at[core, at], own.at[core, i, at], own_sem.at[j, i])

    for j in range(len(groups)):
        own_copy(j, 0).start()
        own_copy(j, 1).start()
    k_rows = pl.ds(pl.multiple_of(mz * tok, tok), tok)
    local_copies = [
        pltpu.make_async_copy(cotan, k_v.at[k_rows], local_sem.at[0]),
        pltpu.make_async_copy(weights, w_v, local_sem.at[1]),
        pltpu.make_async_copy(grad, g_v, local_sem.at[2]),
        pltpu.make_async_copy(momentum, m_v, local_sem.at[3]),
        pltpu.make_async_copy(acts, a_v, local_sem.at[4]),
    ]

    low, high = jnp.minimum(x_chip, y_chip), jnp.maximum(x_chip, y_chip)
    low_closed = partner[2 * low] == 2 * low + 1
    high_closed = partner[2 * high] == 2 * high + 1

    def route(i):
        j = partner[i]
        there = lax.div(j, 2)
        first = lax.rem(jnp.where(there < chip, j, i), 2)
        by_high = jnp.logical_and(high_closed,
                                  jnp.logical_or(jnp.logical_not(low_closed), first == 1))
        by = jnp.where(by_high, high, low)
        corner = jnp.where(by == x_chip, 3, 4)
        return jnp.where(there == chip, 0,
                         jnp.where(there == x_chip, 1, jnp.where(there == y_chip, 2, corner)))

    def starts_x(code):
        return jnp.logical_or(code == 1, code == 3)

    def starts_y(code):
        return jnp.logical_or(code == 2, code == 4)

    code0, code1 = route(2 * chip), route(2 * chip + 1)
    code_me, code_twin = route(me), route(twin)

    pl.semaphore_wait(barrier, 3 + p - 1)

    def pair(j, i):
        at = pl.ds(groups[j][0], groups[j][1])
        return remote(pieces[i].at[1 - core, at], own.at[core, i, at],
                      pair_send.at[j, i], pair_recv.at[j, i], replica=twin)

    def pair_in(j, i):
        at = pl.ds(groups[j][0], groups[j][1])
        return remote(pieces[i].at[1 - core, at], own.at[1 - core, i, at],
                      pair_send.at[j, i], pair_recv.at[j, i], replica=twin)

    def link_x(t):
        return remote(tx.at[t], rx.at[t], x_send.at[t], x_recv.at[t], replica=x_dev)

    def link_y(t):
        return remote(ty.at[t], ry.at[t], y_send.at[t], y_recv.at[t], replica=y_dev)

    def hand(c):
        return remote(handed.at[c], taken.at[c], hand_send.at[c], hand_recv.at[c], replica=twin)

    def share(to):
        return remote(cotan, k_v.at[k_rows], k_send.at[to], k_recv.at[mz], fsdp=to)

    def share_in(frm):
        rows = pl.ds(pl.multiple_of(frm * tok, tok), tok)
        return remote(cotan, k_v.at[rows], k_send.at[frm], k_recv.at[frm], fsdp=frm)

    for j in range(len(groups)):
        pair(j, 0).start()
        pair(j, 1).start()
        if j == 0:
            @pl.loop(1, p)
            def _(d):
                share(lax.rem(mz + d, p)).start()

    def pick(code, near, c):
        far = lax.select(code == 3, rx[c + DELAY], ry[c + DELAY])
        far = lax.select(code == 2, ry[c], far)
        far = lax.select(code == 1, rx[c], far)
        return lax.select(code == 0, near, far)

    out_copies = []

    def settle(half, c, got):
        nw_v[half, c], nm_v[half, c] = update(
            w_v[half, c], g_v[half, c], m_v[half, c], got[0], got[1])

    def finish(c):
        hand(c).wait_recv()
        settle(1 - core, c, taken[c])
        if c % GROUP == GROUP - 1:
            at = pl.ds(c - GROUP + 1, GROUP)
            for i, (src, dst) in enumerate(((nw_v, new_weights), (nm_v, new_momentum))):
                cp = pltpu.make_async_copy(src.at[:, at], dst.at[:, at], out_sem.at[i, c // GROUP])
                cp.start()
                out_copies.append(cp)

    def deliver(c):
        handed[c] = pick(code_twin, own[core, :, c], c)
        hand(c).start()
        settle(core, c, pick(code_me, own[1 - core, :, c], c))
        if c >= LAG:
            finish(c - LAG)

    for t in range(chunks + DELAY):
        for j, (at, _) in enumerate(groups):
            if at == t:
                for i in range(2):
                    own_copy(j, i).wait()
                    pair_in(j, i).wait_recv()
        if t < chunks:
            block0, block1 = own[0, :, t], own[1, :, t]
        if t >= DELAY:
            link_x(t - DELAY).wait_recv()
            link_y(t - DELAY).wait_recv()
            out_x, out_y = ry[t - DELAY], rx[t - DELAY]
        else:
            out_x, out_y = block1, block1
        if t < chunks:
            out_x = lax.select(starts_x(code0), block0, lax.select(starts_x(code1), block1, out_x))
            out_y = lax.select(starts_y(code0), block0, lax.select(starts_y(code1), block1, out_y))
        tx[t] = out_x
        link_x(t).start()
        ty[t] = out_y
        link_y(t).start()
        if t == 1:
            for cp in local_copies:
                cp.start()
        if t == 2 * DELAY:
            for cp in local_copies:
                cp.wait()
        if t >= 2 * DELAY:
            deliver(t - 2 * DELAY)

    @pl.loop(1, p)
    def _(d):
        share_in(lax.rem(mz + p - d, p)).wait_recv()

    def tile_out(tile):
        multiply(a_v, k_v, wg_v, tile)
        step = a_v.shape[1] // TILES
        at = pl.ds(tile * step, step)
        cp = pltpu.make_async_copy(wg_v.at[at], weight_grad.at[at], out_sem.at[2, tile])
        cp.start()
        out_copies.append(cp)

    tile_out(0)
    tile_out(1)
    for t in range(chunks, chunks + DELAY):
        link_x(t).wait_recv()
        link_y(t).wait_recv()
        deliver(t - DELAY)
        if t < chunks + 2:
            tile_out(2 + t - chunks)
    for c in range(chunks - LAG, chunks):
        finish(c)

    for t in range(chunks + DELAY):
        link_x(t).wait_send()
        link_y(t).wait_send()
    for c in range(chunks):
        hand(c).wait_send()
    for j in range(len(groups)):
        pair(j, 0).wait_send()
        pair(j, 1).wait_send()

    @pl.loop(1, p)
    def _(d):
        share(lax.rem(mz + d, p)).wait_send()

    for cp in out_copies:
        cp.wait()


def call(body, identity, view, operands, scratch):
    partner, weights, grad, momentum, acts, cotan = operands
    bf16 = jnp.bfloat16
    (tokens, feats), cols = acts.shape, cotan.shape[1]
    out_view = jax.ShapeDtypeStruct(view, bf16)
    any_space = pl.BlockSpec(memory_space=pl.ANY)
    return pl.pallas_call(
        body,
        out_shape=(out_view, out_view, jax.ShapeDtypeStruct((feats, cols), bf16)),
        in_specs=[pl.BlockSpec(memory_space=pltpu.SMEM)]
        + [pl.BlockSpec(memory_space=pltpu.HBM)] * 5,
        out_specs=(any_space,) * 3,
        scratch_shapes=scratch,
        compiler_params=pltpu.CompilerParams(
            collective_id=identity, has_side_effects=True, vmem_limit_bytes=32 * MIB),
        cost_estimate=pl.CostEstimate(
            flops=2 * tokens * feats * cols, bytes_accessed=20 * weights.size // weights.shape[0],
            transcendentals=0),
    )(partner, weights.reshape(view), grad.reshape(view), momentum.reshape(view), acts, cotan)


def spread_form(n, p, weights, pseudo_grad, momentum, partner, activations, key_cotangent):
    rows, cols = weights.shape
    chunks = CHUNKS if rows >= n * CHUNKS * ROW_TILE else 1
    piece = -(-rows // (n * chunks * ROW_TILE)) * ROW_TILE
    padded = n * chunks * piece
    view = (n, chunks, piece, cols)

    def cut(x):
        return jnp.pad(x, ((0, padded - rows), (0, 0))) if padded != rows else x

    def join(x):
        return x.reshape(padded, cols)[:rows]

    bf16 = jnp.bfloat16
    tokens, feats = activations.shape
    dma = pltpu.SemaphoreType.DMA
    vmem = pltpu.VMEM
    scratch = [vmem((2, n, piece, cols), bf16) for _ in range(chunks)] + [
        vmem((chunks, n, 2, piece, cols), bf16), vmem((chunks, n, 2, piece, cols), bf16),
        vmem(view, bf16), vmem(view, bf16), vmem(view, bf16),
        vmem((tokens, feats), bf16), vmem((tokens, cols), bf16),
        vmem(view, bf16), vmem(view, bf16), vmem((feats, cols), bf16),
        dma((chunks, 2, n)), dma((chunks, 2, n)), dma((chunks, n)), dma((chunks, n)),
        dma((p,)), dma((p,)), dma((5,)), dma((chunks, 2)), dma((3, chunks)),
    ]
    new_weights, new_momentum, weight_grad = call(
        functools.partial(kernel, n, p, chunks), 0, view,
        (partner, cut(weights), cut(pseudo_grad), cut(momentum), activations, key_cotangent),
        scratch)
    return join(new_weights), join(new_momentum), weight_grad


def lane_form(p, weights, pseudo_grad, momentum, partner, activations, key_cotangent):
    rows, cols = weights.shape
    chunks = LANE_CHUNKS
    piece = rows // (2 * chunks)
    view = (2, chunks, piece, cols)
    groups = ((0, 2), (2, 2), (4, 4), (8, 8), (16, chunks - 16))
    bf16 = jnp.bfloat16
    tokens, feats = activations.shape
    dma = pltpu.SemaphoreType.DMA
    vmem = pltpu.VMEM
    lane = vmem((chunks + DELAY, 2, piece, cols), bf16)
    scratch = [
        vmem((2, 2, chunks, piece, cols), bf16), lane, lane, lane, lane,
        vmem((chunks, 2, piece, cols), bf16), vmem((chunks, 2, piece, cols), bf16),
        vmem(view, bf16), vmem(view, bf16), vmem(view, bf16),
        vmem((tokens, feats), bf16), vmem((tokens, cols), bf16),
        vmem(view, bf16), vmem(view, bf16), vmem((feats, cols), bf16),
        *[dma((chunks + DELAY,))] * 4,
        dma((len(groups), 2)), dma((len(groups), 2)), dma((chunks,)), dma((chunks,)),
        dma((p,)), dma((p,)), dma((5,)), dma((len(groups), 2)), dma((3, chunks // GROUP)),
    ]
    new_weights, new_momentum, weight_grad = call(
        functools.partial(lane_kernel, p, chunks, groups), 1, view,
        (partner, weights, pseudo_grad, momentum, activations, key_cotangent), scratch)
    return new_weights.reshape(rows, cols), new_momentum.reshape(rows, cols), weight_grad


def publish(arrays):
    parts = 2
    count = len(arrays)

    def body(*refs):
        sources, targets, sem = refs[:count], refs[count:2 * count], refs[-1]
        copies = []
        for i, (source, target) in enumerate(zip(sources, targets)):
            size = source.shape[0] // parts
            for j in range(parts):
                at = pl.ds(j * size, size)
                copies.append(pltpu.make_async_copy(source.at[at], target.at[at], sem.at[i, j]))
        for cp in copies:
            cp.start()
        for cp in copies:
            cp.wait()

    any_space = pl.BlockSpec(memory_space=pl.ANY)
    total = sum(2 * x.size * x.dtype.itemsize for x in arrays)
    return pl.pallas_call(
        body,
        out_shape=tuple(jax.ShapeDtypeStruct(x.shape, x.dtype) for x in arrays),
        in_specs=[pl.BlockSpec(memory_space=pltpu.VMEM)] * count,
        out_specs=(any_space,) * count,
        scratch_shapes=[pltpu.SemaphoreType.DMA((count, parts))],
        compiler_params=pltpu.CompilerParams(vmem_limit_bytes=16 * MIB),
        cost_estimate=pl.CostEstimate(flops=0, bytes_accessed=total, transcendentals=0),
    )(*arrays)


def one_block_a_link(partner):
    index = lax.iota(jnp.int32, 8)
    over_x = (index // 2 + partner // 2) % 2
    over_y = (index // 4 + partner // 4) % 2
    crossings = jnp.sum(over_x + 16 * over_y)
    return (crossings == 0) | (crossings == 4 * 17)


def on_device(weights, pseudo_grad, momentum, partner, activations, key_cotangent):
    n, p = lax.axis_size("replica"), lax.axis_size("fsdp")
    operands = (weights[0], pseudo_grad[0], momentum[0], partner, activations, key_cotangent)
    spread = functools.partial(spread_form, n, p)
    if n == 8 and weights.shape[1] % (2 * LANE_CHUNKS * ROW_TILE) == 0:
        outs = lax.cond(one_block_a_link(partner), functools.partial(lane_form, p), spread,
                        *operands)
    else:
        outs = spread(*operands)
    return tuple(out[None] for out in publish(outs))


def solution(mesh):
    return jax.shard_map(
        on_device,
        mesh=mesh,
        in_specs=(
            P("replica", "fsdp", None),
            P("replica", "fsdp", None),
            P("replica", "fsdp", None),
            P(),
            P("replica", "fsdp"),
            P(("replica", "fsdp"), None),
        ),
        out_specs=(
            P("replica", "fsdp", None),
            P("replica", "fsdp", None),
            P("replica", "fsdp", None),
        ),
        check_vma=False,
    )
```
